512 devices in a mesh: front: 4 (over x), helper: 128 (over y, z, core).
Axes of the slice: x: 4, y: 8, z: 8, core: 2. Of those that a mesh axis runs over, the one named last changes fastest.
Arguments:
- lower_panel: bfloat16 [8192, 2048], P(('front', 'helper')), parts along dimension 0, may hold values from -0.125 to 0.125
- pivot_inverse: bfloat16 [64, 128, 128], P('front'), parts along dimension 0
- lower_rows: bfloat16 [131072, 2048], P(('front', 'helper')), parts along dimension 0, may hold values from -1 to 1
- window_block: bfloat16 [131072, 512], P(('front', 'helper')), parts along dimension 0, may hold values from -6 to 6
- block_count: int32 [512], P(('front', 'helper')), parts along dimension 0, may hold values from 1 to 2, as said below
- parent_slot: int32 [131072], P(('front', 'helper')), parts along dimension 0, may hold values from 0 to 16383, as said below
Outputs:
- factor_rows: bfloat16 [131072, 2048], P(('front', 'helper')), parts along dimension 0
- parent_block: float32 [65536, 512], P(('front', 'helper')), parts along dimension 0
The draws below stay inside these ranges and needn't reach their ends.
There are 4 independent parts, one for each index of `front`. The reference program is written for one: setup_inputs(seed, part) draws one part's arguments, and reference() takes and returns one part's arrays. A program takes and returns all parts, laid end to end along the dimension named above; each array names one. Nothing has to cross between parts.
Inputs may be any that keep to these rules, and one draw needn't show every extreme that they name: `block_count`: each helper holds 1 to 2 blocks; some helper holds 2. Owner is parent_slot // 128. The 256 slots of one helper name each owner at most 2 times; in every draw one owner is named by the first 2 slots of every helper.
All inputs are finite; a program needn't handle non-finite values.
Results may differ from the reference program's by a relative error of at most 0.0062.
Values may be sent and summed in bfloat16 or wider, within the bound.
No kernel may reach another device: no remote copies, remote signals or barrier semaphores. Data moves between devices by JAX's collectives and lax.ppermute only.
A program may use at most 64 MiB of HBM per device.

```python
import jax
import jax.numpy as jnp
from jax import lax

NPIV = 2048
BS = 128
UNIT = 128
MAXB = 2
SR = 4
PROWS = 128
NB = 16
ROWS_DEV = 256
ROWS_TOTAL = 32768
SLAB = 512
CAP = 2
PARENT_ROWS = 16384
N_HELPER = 128


def draw_pivot_inverse(key, part):
    key = jax.random.fold_in(key, 23)
    first, second = jax.random.split(key)
    noise = jax.random.normal(first, (NB, BS, BS), jnp.float32) * (0.5 / BS ** 0.5)
    symmetric = (noise + jnp.swapaxes(noise, 1, 2)) * 0.7071
    diagonal = jax.random.uniform(second, (NB, BS), jnp.float32, 0.5, 2.0)
    eye_block = jnp.eye(BS, dtype=jnp.float32)
    return (symmetric + diagonal[:, :, None] * eye_block[None]).astype(jnp.bfloat16)


def draw_block_count(key, part):
    key = jax.random.fold_in(key, 11)
    first, second = jax.random.split(key)
    helpers = ROWS_TOTAL // ROWS_DEV
    counts = jax.random.randint(first, (helpers,), 1, MAXB + 1)
    fullest = jax.random.randint(second, (), 0, helpers)
    counts = jnp.where(jnp.arange(helpers) == fullest, MAXB, counts)
    return counts.astype(jnp.int32)


def draw_parent_slot(key, part):
    key = jax.random.fold_in(key, 37)
    first, second, third = jax.random.split(key, 3)
    helpers = ROWS_TOTAL // ROWS_DEV
    common = jax.random.randint(first, (), 0, helpers)
    row_keys = jax.random.split(second, helpers)
    orders = jax.vmap(lambda sub: jax.random.permutation(sub, (helpers - 1) * CAP))(row_keys)
    others = (common + 1 + orders[:, :ROWS_DEV - CAP] // CAP) % helpers
    owners = jnp.concatenate([jnp.full((helpers, CAP), common, jnp.int32), others.astype(jnp.int32)], axis=1)
    local_row = jax.random.randint(third, (helpers, ROWS_DEV), 0, PROWS)
    return (owners * PROWS + local_row).reshape(-1).astype(jnp.int32)


def block_scale(stream_key, dims, cuts, least, largest):
    loudness = 1.0
    for dim, blocks in cuts:
        heights = jax.random.uniform(jax.random.fold_in(jax.random.fold_in(stream_key, 6), dim), (blocks,), jnp.float32, least / len(cuts), largest / len(cuts))
        loudness = loudness * jnp.repeat(jnp.exp(heights), dims[dim] // blocks).reshape((-1,) + (1,) * (len(dims) - 1 - dim))
    return loudness


def centred(rng, dims, scale, bound, cuts=(), kind=jnp.bfloat16):
    array = scale * jax.random.normal(rng, dims, jnp.float32)
    if cuts:
        array = array * block_scale(rng, dims, cuts, -0.22, 0.18)
    return jnp.clip(array, -bound, bound).astype(kind)


def setup_inputs(seed: int = 0, part: int = 0) -> dict:
    key_list = jax.random.split(jax.random.key(seed), 7)
    part_splits = jax.random.split(jax.random.fold_in(key_list[6], part), 7)
    lower_panel = centred(part_splits[0], (NPIV, NPIV), NPIV ** -0.5, 0.125, ((0, 128),))
    pivot_inverse = draw_pivot_inverse(jax.random.fold_in(jax.random.fold_in(key_list[6], part), 71), part)
    lower_rows = centred(part_splits[2], (ROWS_TOTAL, NPIV), 0.125, 1.0, ((0, 128),))
    window_block = centred(part_splits[3], (ROWS_TOTAL, SLAB), 1.0, 6.0, ((0, 128),))
    block_count = draw_block_count(jax.random.fold_in(jax.random.fold_in(key_list[6], part), 71), part)
    parent_slot = draw_parent_slot(jax.random.fold_in(jax.random.fold_in(key_list[6], part), 71), part)
    return dict(lower_panel=lower_panel, pivot_inverse=pivot_inverse, lower_rows=lower_rows, window_block=window_block, block_count=block_count, parent_slot=parent_slot)


def solve_rows(row_block, pivot_panel, inverse):
    count_blocks = inverse.shape[0]
    block_width = inverse.shape[1]
    pieces = []
    for block_index in range(count_blocks):
        column_start = block_index * block_width
        current = row_block[:, column_start:column_start + block_width].astype(jnp.float32)
        if block_index > 0:
            earlier = jnp.concatenate(pieces, axis=1)
            current = current - lax.dot_general(earlier, pivot_panel[column_start:column_start + block_width, :column_start], (((1,), (1,)), ((), ())), preferred_element_type=jnp.float32)
        pieces.append(current.astype(jnp.bfloat16))
    solved = jnp.concatenate(pieces, axis=1)
    shaped = solved.reshape(solved.shape[0], count_blocks, block_width).astype(jnp.float32)
    factor = jnp.einsum("rkb,kbc->rkc", shaped, inverse.astype(jnp.float32))
    return solved, factor.reshape(solved.shape).astype(jnp.bfloat16)


def reference(lower_panel, pivot_inverse, lower_rows, window_block, block_count, parent_slot):
    solved, factor = solve_rows(lower_rows, lower_panel, pivot_inverse)
    position = jnp.arange(ROWS_TOTAL, dtype=jnp.int32)
    limit = UNIT * jnp.repeat(block_count, ROWS_DEV)
    live_rows = (position % ROWS_DEV) < limit
    factor = jnp.where(live_rows[:, None], factor, jnp.zeros_like(factor))
    window_rows = factor.reshape(N_HELPER, ROWS_DEV, NPIV)[:, :SR].reshape(SLAB, NPIV)
    product = lax.dot_general(solved, window_rows, (((1,), (1,)), ((), ())), preferred_element_type=jnp.float32)
    contribution = (window_block.astype(jnp.float32) - product).astype(jnp.bfloat16)
    target = jnp.where(live_rows, parent_slot, PARENT_ROWS).astype(jnp.int32)
    parent_block = jnp.zeros((PARENT_ROWS, SLAB), jnp.float32).at[target].add(contribution.astype(jnp.float32), mode="drop")
    return factor, parent_block
```

```python
import functools

import jax
import jax.numpy as jnp
from jax import lax
from jax.experimental import pallas as pl
from jax.experimental.pallas import tpu as pltpu
from jax.sharding import PartitionSpec as P

UNIT = 128
SR = 4
PROWS = 128
BS = 128
NB = 16
NPIV = 2048
ROWS = 256
SLAB = 512
HELPERS = 128
CAP = 2
SLOTS = HELPERS * CAP
WIDE = SLAB + 128
ALL = SLAB + ROWS
F32 = jnp.float32
BF16 = jnp.bfloat16
NT = (((1,), (1,)), ((), ()))
TN = (((0,), (0,)), ((), ()))


def dot(a, b, dims=(((1,), (0,)), ((), ()))):
    return lax.dot_general(a, b, dims, preferred_element_type=F32)


def front_kernel(
    count_ref, panel_hbm, window_hbm, rows_ref, block_ref, inv_ref, slot_ref,
    factor_ref, send_ref, lt, xw, solved, wfac, sems,
):
    copies = [pltpu.make_async_copy(window_hbm, xw, sems.at[0])]
    steps = NB // 2
    per_step = [[] for _ in range(steps)]
    for s in range(steps):
        for j in range(2 * s + 1):
            top = 256 * s if j < 2 * s else 256 * s + BS
            rows = pl.ds(top, 256 * (s + 1) - top)
            per_step[s].append(
                pltpu.make_async_copy(
                    panel_hbm.at[rows, pl.ds(BS * j, BS)], lt.at[j, rows, :], sems.at[1 + s]
                )
            )
    for c in copies:
        c.start()
    for group in per_step:
        for c in group:
            c.start()

    live_count = UNIT * count_ref[0]
    live = lax.broadcasted_iota(jnp.int32, (ROWS, 1), 0) < live_count

    for c in copies:
        c.wait()
    for s in range(steps):
        for c in per_step[s]:
            c.wait()
        lo = 256 * s
        k0, k1 = 2 * s, 2 * s + 1
        x0 = jnp.concatenate([xw[k0], rows_ref[:, lo : lo + BS]], axis=0).astype(F32)
        x1 = jnp.concatenate([xw[k1], rows_ref[:, lo + BS : lo + 256]], axis=0).astype(F32)
        if s > 0:
            panel = jnp.concatenate([lt[j, lo : lo + 256, :] for j in range(k0)], axis=1)
            update = dot(solved[:, :lo], panel, NT)
            x0 = x0 - update[:, :BS]
            x1 = x1 - update[:, BS:]
        s0 = x0.astype(BF16)
        x1 = x1 - dot(s0, lt[k0, lo + BS : lo + 256, :], NT)
        s1 = x1.astype(BF16)
        solved[:, lo : lo + BS] = s0
        solved[:, lo + BS : lo + 256] = s1
        for part, base in ((s0, lo), (s1, lo + BS)):
            f = dot(part, inv_ref[base // BS]).astype(BF16)
            wfac[:, base : base + BS] = f[:SLAB]
            factor_ref[:, base : base + BS] = jnp.where(live, f[SLAB:], jnp.zeros((), BF16))

    product = dot(solved[SLAB:, :], wfac[...], NT)
    contribution = (block_ref[...].astype(F32) - product).astype(BF16)

    slot = slot_ref[...]
    owner_row = jnp.broadcast_to(lax.shift_right_logical(slot, 7).astype(F32), (ROWS, ROWS))
    owner_col = owner_row.T
    local_row = jnp.broadcast_to((slot & 127).astype(F32) + 1.0, (BS, ROWS))
    local_col = local_row.T.astype(BF16)
    i0 = lax.broadcasted_iota(jnp.int32, (ROWS, ROWS), 0)
    i1 = lax.broadcasted_iota(jnp.int32, (ROWS, ROWS), 1)
    earlier = jnp.where((owner_row == owner_col) & (i0 < i1) & (i0 < live_count), 1.0, 0.0)
    rank = jnp.sum(earlier, axis=0, keepdims=True)
    target = owner_row * CAP + rank
    chosen = jnp.where((target == i0.astype(F32)) & (i1 < live_count), 1.0, 0.0).astype(BF16)
    payload = jnp.concatenate([contribution, local_col], axis=1)
    send_ref[...] = dot(chosen, payload).astype(BF16)


def front_call(panel, window, rows, block, inverse, count, slot):
    vmem = pl.BlockSpec(memory_space=pltpu.VMEM)
    hbm = pl.BlockSpec(memory_space=pl.ANY)
    return pl.pallas_call(
        front_kernel,
        out_shape=(
            jax.ShapeDtypeStruct((ROWS, NPIV), BF16),
            jax.ShapeDtypeStruct((SLOTS, WIDE), BF16),
        ),
        in_specs=[pl.BlockSpec(memory_space=pltpu.SMEM), hbm, hbm, vmem, vmem, vmem, vmem],
        out_specs=(vmem, vmem),
        scratch_shapes=[
            pltpu.VMEM((NB, NPIV, BS), BF16),
            pltpu.VMEM((NB, SLAB, BS), BF16),
            pltpu.VMEM((ALL, NPIV), BF16),
            pltpu.VMEM((SLAB, NPIV), BF16),
            pltpu.SemaphoreType.DMA((1 + NB // 2,)),
        ],
        compiler_params=pltpu.CompilerParams(vmem_limit_bytes=50 * 1024 * 1024),
        name="front",
    )(count, panel, window, rows, block, inverse, slot)


def assemble_kernel(got_ref, out_ref):
    got = got_ref[...]
    local = got[:, SLAB:].astype(F32)
    wanted = lax.broadcasted_iota(jnp.int32, (SLOTS, PROWS), 1).astype(F32) + 1.0
    chooser = jnp.where(local == wanted, 1.0, 0.0).astype(BF16)
    out_ref[...] = dot(chooser, got[:, :SLAB], TN)


def assemble_call(got):
    vmem = pl.BlockSpec(memory_space=pltpu.VMEM)
    return pl.pallas_call(
        assemble_kernel,
        out_shape=jax.ShapeDtypeStruct((PROWS, SLAB), F32),
        in_specs=[vmem],
        out_specs=vmem,
        name="assemble",
    )(got)


def per_device(lower_panel, pivot_inverse, lower_rows, window_block, block_count, parent_slot):
    mine = jnp.concatenate([lower_panel, lower_rows[:SR]], axis=0)
    every = lax.all_gather(mine, "helper", axis=0)
    panel = every[:, :16].reshape(NPIV, NPIV)
    window = every[:, 16:].reshape(SLAB, NB, BS).transpose(1, 0, 2)
    factor, send = front_call(
        panel, window, lower_rows, window_block, pivot_inverse, block_count, parent_slot.reshape(1, ROWS)
    )
    got = lax.all_to_all(
        send.reshape(HELPERS, CAP, WIDE), "helper", split_axis=0, concat_axis=0, tiled=True
    )
    return factor, assemble_call(got.reshape(SLOTS, WIDE))


def solution(mesh):
    return jax.shard_map(
        per_device,
        mesh=mesh,
        in_specs=(
            P(("front", "helper"), None),
            P("front", None, None),
            P(("front", "helper"), None),
            P(("front", "helper"), None),
            P(("front", "helper")),
            P(("front", "helper")),
        ),
        out_specs=(P(("front", "helper"), None), P(("front", "helper"), None)),
        check_vma=False,
    )
```

```python
import functools

import jax
import jax.numpy as jnp
from jax import lax
from jax.experimental import pallas as pl
from jax.experimental.pallas import tpu as pltpu
from jax.sharding import PartitionSpec as P

UNIT = 128
SR = 4
PROWS = 128
BS = 128
NB = 16
NPIV = 2048
ROWS = 256
SLAB = 512
HELPERS = 128
CAP = 2
SLOTS = HELPERS * CAP
WIDE = SLAB + 128
ALL = SLAB + ROWS
F32 = jnp.float32
BF16 = jnp.bfloat16
NT = (((1,), (1,)), ((), ()))
TN = (((0,), (0,)), ((), ()))
LINE = 8
PAIRS = 4
SENT = NB - 1 + SR
PIECES = PAIRS * NB + 2 * NB
FROM = (0, 2, -2, 1, 3, -1, -3, 4)


def helper(y, z, core):
    return 2 * LINE * y + 2 * z + core


def line_groups():
    return [[helper(y, z, 0) for y in range(LINE)] for z in range(LINE)] + [
        [helper(g if z % 2 == 0 else 7 - g, z, 1) for z in range(LINE)] for g in range(LINE)
    ]


def from_offset(step):
    pairs = []
    for y in range(LINE):
        for z in range(LINE):
            pairs.append((helper(y, (z + step) % LINE, 0), helper(y, z, 0)))
            pairs.append((helper((y + step) % LINE, z, 1), helper(y, z, 1)))
    return pairs


def place():
    me = lax.axis_index("helper")
    return lax.div(me, 16), lax.rem(lax.div(me, 2), 8), lax.rem(me, 2)


def dot(a, b, dims=(((1,), (0,)), ((), ()))):
    return lax.dot_general(a, b, dims, preferred_element_type=F32)


def spread_kernel(panel_ref, rows_ref, out_ref, window):
    for j in range(NB):
        window[SR * j : SR * (j + 1), :] = rows_ref[:, BS * j : BS * (j + 1)].astype(F32)[:SR]
    leading = window[...].astype(BF16).reshape(SR, 16, BS)
    for d in range(LINE):
        for j in range(NB - 1):
            out_ref[d, j] = panel_ref[:, BS * j : BS * (j + 1)]
        out_ref[d, NB - 1 :] = leading


def spread_call(panel, rows):
    return pl.pallas_call(
        spread_kernel,
        grid=(1,),
        out_shape=jax.ShapeDtypeStruct((LINE, SENT, 16, BS), BF16),
        in_specs=[pl.BlockSpec((16, NPIV), lambda i: (0, 0))] * 2,
        out_specs=pl.BlockSpec((LINE, SENT, 16, BS), lambda i: (0, 0, 0, 0)),
        scratch_shapes=[pltpu.VMEM((SR * NB, BS), F32)],
        name="spread",
    )(panel, rows)


def pack_kernel(line_ref, out_ref, window):
    y, z, core = place()
    label = jnp.where(lax.rem(z, 2) == 0, y, 7 - y)
    low = jnp.minimum(label, 7 - label)
    for p in range(PAIRS):
        upper = jnp.where(core == 0, jnp.where(z >= 4, 1, 0), 1 if p >= 2 else 0)
        first = jnp.where(core == 0, p, low)
        count = 14 - 2 * first + upper
        swap = jnp.where(label <= 3, 0, 1)
        large = jnp.where(core == 0, 7 - p, 2 * p + 1 - swap)
        small = jnp.where(core == 0, p, 2 * p + swap)
        for s in range(NB):
            member = jnp.where(s < count, large, small)
            piece = jnp.where(s < count, s, s - count)
            out_ref[NB * p + s] = line_ref[member, piece]
    for d in range(LINE):
        leading = line_ref[d, NB - 1 :].astype(F32)
        for j in range(NB):
            window[j, SR * d : SR * (d + 1), :] = leading[j // 4, SR * (j % 4) : SR * (j % 4 + 1), :]
    out_ref[PAIRS * NB :] = window[...].astype(BF16).reshape(2 * NB, 16, BS)


def pack_call(line):
    vmem = pl.BlockSpec(memory_space=pltpu.VMEM)
    return pl.pallas_call(
        pack_kernel,
        out_shape=jax.ShapeDtypeStruct((PIECES, 16, BS), BF16),
        in_specs=[vmem],
        out_specs=vmem,
        scratch_shapes=[pltpu.VMEM((NB, SR * LINE, BS), F32)],
        name="pack",
    )(line)


def block_copies(source, core, y, z, lt, xw, sem):
    copies = []
    label_sign = lax.rem(z, 2) == 0
    for q, step in enumerate(FROM):
        base = PIECES * q
        if core == 0:
            member = lax.rem(z + step + LINE, LINE)
            window_row = 32 * member
        else:
            other = lax.rem(y + step + LINE, LINE)
            member = jnp.where(label_sign, other, 7 - other)
            window_row = 32 * member + SLAB // 2
        copies.append(
            pltpu.make_async_copy(
                source.at[pl.ds(base + PAIRS * NB, 2 * NB)], xw.at[lax.div(window_row, 32)], sem
            )
        )
        for p in range(PAIRS):
            if core == 0:
                upper = jnp.where(member >= 4, 1, 0)
                count = 14 - 2 * p + upper
                large = helper(7 - p, member, 0)
                small = helper(p, member, 0)
            else:
                upper = 1 if p >= 2 else 0
                low = jnp.minimum(member, 7 - member)
                count = 14 - 2 * low + upper
                z_large = jnp.where(member <= 3, 2 * p + 1, 2 * p)
                large = helper(7 - low, z_large, 1)
                small = helper(low, 4 * p + 1 - z_large, 1)
            start = base + NB * p
            copies.append(
                pltpu.make_async_copy(
                    source.at[pl.ds(start, NB)], lt.at[:, large], sem
                )
            )
            copies.append(
                pltpu.make_async_copy(
                    source.at[pl.ds(start + count, NB // 2)], lt.at[pl.ds(0, NB // 2), small], sem
                )
            )
    return copies


def front_kernel(
    count_ref, mine_hbm, other_hbm, rows_ref, block_ref, inv_ref, slot_ref,
    factor_ref, send_ref, lt, xw, solved, wfac, sem,
):
    y, z, core = place()

    def copies(here):
        refs = (mine_hbm, other_hbm) if here == 0 else (other_hbm, mine_hbm)
        return block_copies(refs[0], 0, y, z, lt, xw, sem) + block_copies(refs[1], 1, y, z, lt, xw, sem)

    for here in (0, 1):
        @pl.when(core == here)
        def _():
            for c in copies(here):
                c.start()

    for c in copies(0):
        c.wait()

    live_count = UNIT * count_ref[0]
    live = lax.broadcasted_iota(jnp.int32, (ROWS, 1), 0) < live_count

    def window_piece(k):
        return xw[:, 2 * k : 2 * k + 2].reshape(SLAB, BS)

    def panel_piece(j, top, count):
        return lt[j, top // 16 : (top + count) // 16].reshape(count, BS)

    for s in range(NB // 2):
        lo = 256 * s
        k0, k1 = 2 * s, 2 * s + 1
        x0 = jnp.concatenate([window_piece(k0), rows_ref[:, lo : lo + BS]], axis=0).astype(F32)
        x1 = jnp.concatenate([window_piece(k1), rows_ref[:, lo + BS : lo + 256]], axis=0).astype(F32)
        if s > 0:
            panel = jnp.concatenate([panel_piece(j, lo, 256) for j in range(k0)], axis=1)
            update = dot(solved[:, :lo], panel, NT)
            x0 = x0 - update[:, :BS]
            x1 = x1 - update[:, BS:]
        s0 = x0.astype(BF16)
        x1 = x1 - dot(s0, panel_piece(k0, lo + BS, BS), NT)
        s1 = x1.astype(BF16)
        solved[:, lo : lo + BS] = s0
        solved[:, lo + BS : lo + 256] = s1
        for part, base in ((s0, lo), (s1, lo + BS)):
            f = dot(part, inv_ref[base // BS]).astype(BF16)
            wfac[:, base : base + BS] = f[:SLAB]
            factor_ref[:, base : base + BS] = jnp.where(live, f[SLAB:], jnp.zeros((), BF16))

    held = lax.broadcasted_iota(jnp.int32, (1, SLAB), 1)
    group = lax.shift_right_logical(held, 5) & 7
    turn = lax.shift_right_logical(held, 2) & 7
    first_half = held < SLAB // 2
    held_y = jnp.where(first_half, turn, jnp.where((turn & 1) == 0, group, 7 - group))
    held_z = jnp.where(first_half, group, turn)
    column = 64 * held_y + 8 * held_z + jnp.where(first_half, 0, 4) + (held & 3)
    order = jnp.where(
        lax.broadcasted_iota(jnp.int32, (SLAB, SLAB), 0) == column, 1.0, 0.0
    ).astype(BF16)

    product = dot(solved[SLAB:, :], wfac[...], NT)
    held_contribution = (dot(block_ref[...], order) - product).astype(BF16)
    contribution = dot(held_contribution, order, NT).astype(BF16)

    slot = slot_ref[...]
    owner_row = jnp.broadcast_to(lax.shift_right_logical(slot, 7).astype(F32), (ROWS, ROWS))
    owner_col = owner_row.T
    local_row = jnp.broadcast_to((slot & 127).astype(F32) + 1.0, (BS, ROWS))
    local_col = local_row.T.astype(BF16)
    i0 = lax.broadcasted_iota(jnp.int32, (ROWS, ROWS), 0)
    i1 = lax.broadcasted_iota(jnp.int32, (ROWS, ROWS), 1)
    earlier = jnp.where((owner_row == owner_col) & (i0 < i1) & (i0 < live_count), 1.0, 0.0)
    rank = jnp.sum(earlier, axis=0, keepdims=True)
    target = owner_row * CAP + rank
    chosen = jnp.where((target == i0.astype(F32)) & (i1 < live_count), 1.0, 0.0).astype(BF16)
    payload = jnp.concatenate([contribution, local_col], axis=1)
    send_ref[...] = dot(chosen, payload).astype(BF16)


def front_call(mine, other, rows, block, inverse, count, slot):
    vmem = pl.BlockSpec(memory_space=pltpu.VMEM)
    hbm = pl.BlockSpec(memory_space=pl.ANY)
    return pl.pallas_call(
        front_kernel,
        out_shape=(
            jax.ShapeDtypeStruct((ROWS, NPIV), BF16),
            jax.ShapeDtypeStruct((SLOTS, WIDE), BF16),
        ),
        in_specs=[pl.BlockSpec(memory_space=pltpu.SMEM), hbm, hbm, vmem, vmem, vmem, vmem],
        out_specs=(vmem, vmem),
        scratch_shapes=[
            pltpu.VMEM((NB, HELPERS, 16, BS), BF16),
            pltpu.VMEM((2 * LINE, 2 * NB, 16, BS), BF16),
            pltpu.VMEM((ALL, NPIV), BF16),
            pltpu.VMEM((SLAB, NPIV), BF16),
            pltpu.SemaphoreType.DMA,
        ],
        compiler_params=pltpu.CompilerParams(vmem_limit_bytes=50 * 1024 * 1024),
        name="front",
    )(count, mine, other, rows, block, inverse, slot)


def assemble_kernel(got_ref, out_ref):
    got = got_ref[...]
    local = got[:, SLAB:].astype(F32)
    wanted = lax.broadcasted_iota(jnp.int32, (SLOTS, PROWS), 1).astype(F32) + 1.0
    chooser = jnp.where(local == wanted, 1.0, 0.0).astype(BF16)
    out_ref[...] = dot(chooser, got[:, :SLAB], TN)


def assemble_call(got):
    vmem = pl.BlockSpec(memory_space=pltpu.VMEM)
    return pl.pallas_call(
        assemble_kernel,
        out_shape=jax.ShapeDtypeStruct((PROWS, SLAB), F32),
        in_specs=[vmem],
        out_specs=vmem,
        name="assemble",
    )(got)


def per_device(lower_panel, pivot_inverse, lower_rows, window_block, block_count, parent_slot):
    def receive(block, step):
        return lax.ppermute(block, "helper", from_offset(step))

    line = lax.all_to_all(
        spread_call(lower_panel, lower_rows), "helper", 0, 0, tiled=True, axis_index_groups=line_groups()
    )
    own = pack_call(line)
    half = PIECES // 2
    after = receive(own, 2)
    before = receive(own, -2)
    above = receive(jnp.concatenate([own, after]), 1)
    below = receive(jnp.concatenate([own, before]), -1)
    far = [receive(after[:half], 2), receive(before[half:], -2)]
    mine = jnp.concatenate([own, after, before, above, below] + far)
    other = lax.ppermute(mine, "helper", [(h, h ^ 1) for h in range(HELPERS)])
    factor, send = front_call(
        mine, other, lower_rows, window_block, pivot_inverse, block_count, parent_slot.reshape(1, ROWS)
    )
    got = lax.all_to_all(
        send.reshape(HELPERS, CAP, WIDE), "helper", split_axis=0, concat_axis=0, tiled=True
    )
    return factor, assemble_call(got.reshape(SLOTS, WIDE))


def solution(mesh):
    return jax.shard_map(
        per_device,
        mesh=mesh,
        in_specs=(
            P(("front", "helper"), None),
            P("front", None, None),
            P(("front", "helper"), None),
            P(("front", "helper"), None),
            P(("front", "helper")),
            P(("front", "helper")),
        ),
        out_specs=(P(("front", "helper"), None), P(("front", "helper"), None)),
        check_vma=False,
    )
```

```python
import functools

import jax
import jax.numpy as jnp
from jax import lax
from jax.experimental import pallas as pl
from jax.experimental.pallas import tpu as pltpu
from jax.sharding import PartitionSpec as P

UNIT = 128
SR = 4
PROWS = 128
BS = 128
NB = 16
NPIV = 2048
ROWS = 256
SLAB = 512
HELPERS = 128
CAP = 2
SLOTS = HELPERS * CAP
WIDE = SLAB + 128
ALL = SLAB + ROWS
F32 = jnp.float32
BF16 = jnp.bfloat16
NT = (((1,), (1,)), ((), ()))
TN = (((0,), (0,)), ((), ()))
LINE = 8
PAIRS = 4
SENT = NB - 1 + SR
PIECES = PAIRS * NB + 2 * NB
FROM = (0, 2, -2, 1, 3, -1, -3, 4)


def helper(y, z, core):
    return 2 * LINE * y + 2 * z + core


def line_groups():
    return [[helper(y, z, 0) for y in range(LINE)] for z in range(LINE)] + [
        [helper(g if z % 2 == 0 else 7 - g, z, 1) for z in range(LINE)] for g in range(LINE)
    ]


def from_offset(step):
    pairs = []
    for y in range(LINE):
        for z in range(LINE):
            pairs.append((helper(y, (z + step) % LINE, 0), helper(y, z, 0)))
            pairs.append((helper((y + step) % LINE, z, 1), helper(y, z, 1)))
    return pairs


def place():
    me = lax.axis_index("helper")
    return lax.div(me, 16), lax.rem(lax.div(me, 2), 8), lax.rem(me, 2)


def dot(a, b, dims=(((1,), (0,)), ((), ()))):
    return lax.dot_general(a, b, dims, preferred_element_type=F32)


def spread_kernel(panel_hbm, rows_hbm, out_ref, panel_ref, rows_ref, window, sems):
    panel_copy = pltpu.make_async_copy(panel_hbm, panel_ref, sems.at[0])
    rows_copy = pltpu.make_async_copy(rows_hbm.at[pl.ds(0, 16)], rows_ref, sems.at[1])
    panel_copy.start()
    rows_copy.start()
    panel_copy.wait()
    rows_copy.wait()
    for j in range(NB):
        window[SR * j : SR * (j + 1), :] = rows_ref[:, BS * j : BS * (j + 1)].astype(F32)[:SR]
    leading = window[...].astype(BF16).reshape(SR, 16, BS)
    for d in range(LINE):
        for j in range(NB - 1):
            out_ref[d, j] = panel_ref[:, BS * j : BS * (j + 1)]
        out_ref[d, NB - 1 :] = leading


def spread_call(panel, rows):
    hbm = pl.BlockSpec(memory_space=pltpu.HBM)
    return pl.pallas_call(
        spread_kernel,
        out_shape=jax.ShapeDtypeStruct((LINE, SENT, 16, BS), BF16),
        in_specs=[hbm, hbm],
        out_specs=pl.BlockSpec(memory_space=pltpu.VMEM),
        scratch_shapes=[
            pltpu.VMEM((16, NPIV), BF16),
            pltpu.VMEM((16, NPIV), BF16),
            pltpu.VMEM((SR * NB, BS), F32),
            pltpu.SemaphoreType.DMA((2,)),
        ],
        compiler_params=pltpu.CompilerParams(vmem_limit_bytes=8 * 1024 * 1024),
        name="spread",
    )(panel, rows)


def pack_kernel(line_ref, out_ref, window):
    y, z, core = place()
    label = jnp.where(lax.rem(z, 2) == 0, y, 7 - y)
    low = jnp.minimum(label, 7 - label)
    for p in range(PAIRS):
        upper = jnp.where(core == 0, jnp.where(z >= 4, 1, 0), 1 if p >= 2 else 0)
        first = jnp.where(core == 0, p, low)
        count = 14 - 2 * first + upper
        swap = jnp.where(label <= 3, 0, 1)
        large = jnp.where(core == 0, 7 - p, 2 * p + 1 - swap)
        small = jnp.where(core == 0, p, 2 * p + swap)
        for s in range(NB):
            member = jnp.where(s < count, large, small)
            piece = jnp.where(s < count, s, s - count)
            out_ref[NB * p + s] = line_ref[member, piece]
    for d in range(LINE):
        leading = line_ref[d, NB - 1 :].astype(F32)
        for j in range(NB):
            window[j, SR * d : SR * (d + 1), :] = leading[j // 4, SR * (j % 4) : SR * (j % 4 + 1), :]
    out_ref[PAIRS * NB :] = window[...].astype(BF16).reshape(2 * NB, 16, BS)


def pack_call(line):
    vmem = pl.BlockSpec(memory_space=pltpu.VMEM)
    return pl.pallas_call(
        pack_kernel,
        out_shape=jax.ShapeDtypeStruct((PIECES, 16, BS), BF16),
        in_specs=[vmem],
        out_specs=vmem,
        scratch_shapes=[pltpu.VMEM((NB, SR * LINE, BS), F32)],
        compiler_params=pltpu.CompilerParams(vmem_limit_bytes=8 * 1024 * 1024),
        name="pack",
    )(line)


def held_at(step):
    place_of = jnp.int32(0)
    for q, offset in enumerate(FROM):
        place_of = jnp.where(step == (offset + LINE) % LINE, q, place_of)
    return PIECES * place_of


def put_tiles(first, second, y, z, lt, xw):
    for core, source in ((0, first), (1, second)):
        for member in range(LINE):
            if core == 0:
                base = held_at(lax.rem(member - z + LINE, LINE))
            else:
                at = jnp.where(lax.rem(z, 2) == 0, member, 7 - member)
                base = held_at(lax.rem(at - y + LINE, LINE))
            xw[core * LINE + member] = source[pl.ds(base + PAIRS * NB, 2 * NB)]
            for p in range(PAIRS):
                if core == 0:
                    low, upper = p, member // 4
                    large, small = helper(7 - p, member, 0), helper(p, member, 0)
                else:
                    low, upper = min(member, 7 - member), p // 2
                    z_large = 2 * p + 1 if member <= 3 else 2 * p
                    large, small = helper(7 - low, z_large, 1), helper(low, 4 * p + 1 - z_large, 1)
                count = 14 - 2 * low + upper
                lt[:count, large] = source[pl.ds(base + NB * p, count)]
                rest = 2 * low + upper
                if rest:
                    lt[:rest, small] = source[pl.ds(base + NB * p + count, rest)]


def front_kernel(
    count_ref, mine_ref, other_ref, rows_ref, block_ref, inv_ref, slot_ref,
    factor_ref, send_ref, lt, xw, solved, wfac,
):
    y, z, core = place()

    @pl.when(core == 0)
    def _():
        put_tiles(mine_ref, other_ref, y, z, lt, xw)

    @pl.when(core == 1)
    def _():
        put_tiles(other_ref, mine_ref, y, z, lt, xw)

    live_count = UNIT * count_ref[0]
    live = lax.broadcasted_iota(jnp.int32, (ROWS, 1), 0) < live_count

    def window_piece(k):
        return xw[:, 2 * k : 2 * k + 2].reshape(SLAB, BS)

    def panel_piece(j, top, count):
        return lt[j, top // 16 : (top + count) // 16].reshape(count, BS)

    def start_block(k):
        return jnp.concatenate([window_piece(k), rows_ref[:, BS * k : BS * (k + 1)]], axis=0).astype(F32)

    def scale(part, k):
        f = dot(part, inv_ref[k]).astype(BF16)
        wfac[:, BS * k : BS * (k + 1)] = f[:SLAB]
        factor_ref[:, BS * k : BS * (k + 1)] = jnp.where(live, f[SLAB:], jnp.zeros((), BF16))

    def pair(s):
        return jnp.concatenate([start_block(2 * s), start_block(2 * s + 1)], axis=1)

    pending = pair(0)
    last = None
    for s in range(NB // 2):
        lo = 256 * s
        k0, k1 = 2 * s, 2 * s + 1
        x = pending
        if s > 0:
            panel = jnp.concatenate([panel_piece(j, lo, 256) for j in (k0 - 2, k0 - 1)], axis=1)
            x = x - dot(last, panel, NT)
        s0 = x[:, :BS].astype(BF16)
        if s + 1 < NB // 2:
            pending = pair(s + 1)
            if s > 0:
                panel = jnp.concatenate([panel_piece(j, lo + 256, 256) for j in range(k0)], axis=1)
                pending = pending - dot(solved[:, :lo], panel, NT)
        s1 = (x[:, BS:] - dot(s0, panel_piece(k0, lo + BS, BS), NT)).astype(BF16)
        last = jnp.concatenate([s0, s1], axis=1)
        solved[:, lo : lo + 256] = last
        scale(s0, k0)
        scale(s1, k1)

    held = lax.broadcasted_iota(jnp.int32, (1, SLAB), 1)
    group = lax.shift_right_logical(held, 5) & 7
    turn = lax.shift_right_logical(held, 2) & 7
    first_half = held < SLAB // 2
    held_y = jnp.where(first_half, turn, jnp.where((turn & 1) == 0, group, 7 - group))
    held_z = jnp.where(first_half, group, turn)
    column = 64 * held_y + 8 * held_z + jnp.where(first_half, 0, 4) + (held & 3)
    order = jnp.where(
        lax.broadcasted_iota(jnp.int32, (SLAB, SLAB), 0) == column, 1.0, 0.0
    ).astype(BF16)

    product = dot(solved[SLAB:, :], wfac[...], NT)
    held_contribution = (dot(block_ref[...], order) - product).astype(BF16)
    contribution = dot(held_contribution, order, NT).astype(BF16)

    slot = slot_ref[...]
    owner_row = jnp.broadcast_to(lax.shift_right_logical(slot, 7).astype(F32), (ROWS, ROWS))
    owner_col = owner_row.T
    local_row = jnp.broadcast_to((slot & 127).astype(F32) + 1.0, (BS, ROWS))
    local_col = local_row.T.astype(BF16)
    i0 = lax.broadcasted_iota(jnp.int32, (ROWS, ROWS), 0)
    i1 = lax.broadcasted_iota(jnp.int32, (ROWS, ROWS), 1)
    earlier = jnp.where((owner_row == owner_col) & (i0 < i1) & (i0 < live_count), 1.0, 0.0)
    rank = jnp.sum(earlier, axis=0, keepdims=True)
    target = owner_row * CAP + rank
    chosen = jnp.where((target == i0.astype(F32)) & (i1 < live_count), 1.0, 0.0).astype(BF16)
    payload = jnp.concatenate([contribution, local_col], axis=1)
    send_ref[...] = dot(chosen, payload).astype(BF16)


def front_call(mine, other, rows, block, inverse, count, slot):
    vmem = pl.BlockSpec(memory_space=pltpu.VMEM)
    return pl.pallas_call(
        front_kernel,
        out_shape=(
            jax.ShapeDtypeStruct((ROWS, NPIV), BF16),
            jax.ShapeDtypeStruct((SLOTS, WIDE), BF16),
        ),
        in_specs=[pl.BlockSpec(memory_space=pltpu.SMEM)] + [vmem] * 6,
        out_specs=(vmem, vmem),
        scratch_shapes=[
            pltpu.VMEM((NB, HELPERS, 16, BS), BF16),
            pltpu.VMEM((2 * LINE, 2 * NB, 16, BS), BF16),
            pltpu.VMEM((ALL, NPIV), BF16),
            pltpu.VMEM((SLAB, NPIV), BF16),
        ],
        compiler_params=pltpu.CompilerParams(vmem_limit_bytes=32 * 1024 * 1024),
        name="front",
    )(count, mine, other, rows, block, inverse, slot)


def assemble_kernel(got_ref, out_ref):
    got = got_ref[...]
    local = got[:, SLAB:].astype(F32)
    wanted = lax.broadcasted_iota(jnp.int32, (SLOTS, PROWS), 1).astype(F32) + 1.0
    chooser = jnp.where(local == wanted, 1.0, 0.0).astype(BF16)
    out_ref[...] = dot(chooser, got[:, :SLAB], TN)


def assemble_call(got):
    vmem = pl.BlockSpec(memory_space=pltpu.VMEM)
    return pl.pallas_call(
        assemble_kernel,
        out_shape=jax.ShapeDtypeStruct((PROWS, SLAB), F32),
        in_specs=[vmem],
        out_specs=vmem,
        compiler_params=pltpu.CompilerParams(vmem_limit_bytes=8 * 1024 * 1024),
        name="assemble",
    )(got)


def per_device(lower_panel, pivot_inverse, lower_rows, window_block, block_count, parent_slot):
    def receive(block, step):
        return lax.ppermute(block, "helper", from_offset(step))

    line = lax.all_to_all(
        spread_call(lower_panel, lower_rows), "helper", 0, 0, tiled=True, axis_index_groups=line_groups()
    )
    own = pack_call(line)
    half = PIECES // 2
    after = receive(own, 2)
    before = receive(own, -2)
    above = receive(jnp.concatenate([own, after]), 1)
    below = receive(jnp.concatenate([own, before]), -1)
    far = [receive(after[:half], 2), receive(before[half:], -2)]
    mine = jnp.concatenate([own, after, before, above, below] + far)
    other = lax.ppermute(mine, "helper", [(h, h ^ 1) for h in range(HELPERS)])
    factor, send = front_call(
        mine, other, lower_rows, window_block, pivot_inverse, block_count, parent_slot.reshape(1, ROWS)
    )
    got = lax.all_to_all(
        send.reshape(HELPERS, CAP, WIDE), "helper", split_axis=0, concat_axis=0, tiled=True
    )
    return factor, assemble_call(got.reshape(SLOTS, WIDE))


def solution(mesh):
    return jax.shard_map(
        per_device,
        mesh=mesh,
        in_specs=(
            P(("front", "helper"), None),
            P("front", None, None),
            P(("front", "helper"), None),
            P(("front", "helper"), None),
            P(("front", "helper")),
            P(("front", "helper")),
        ),
        out_specs=(P(("front", "helper"), None), P(("front", "helper"), None)),
        check_vma=False,
    )
```

```python
import functools

import jax
import jax.numpy as jnp
from jax import lax
from jax.experimental import pallas as pl
from jax.experimental.pallas import tpu as pltpu
from jax.sharding import PartitionSpec as P

UNIT = 128
SR = 4
PROWS = 128
BS = 128
NB = 16
NPIV = 2048
ROWS = 256
SLAB = 512
HELPERS = 128
CAP = 2
SLOTS = HELPERS * CAP
WIDE = SLAB + 128
ALL = SLAB + ROWS
F32 = jnp.float32
BF16 = jnp.bfloat16
NT = (((1,), (1,)), ((), ()))
TN = (((0,), (0,)), ((), ()))
LINE = 8
PAIRS = 4
SENT = NB - 1 + SR
PIECES = PAIRS * NB + 2 * NB
FROM = (0, 1, -1, 2, -2, 3, -3, 4)


def helper(y, z, core):
    return 2 * LINE * y + 2 * z + core


def line_groups():
    return [[helper(y, z, 0) for y in range(LINE)] for z in range(LINE)] + [
        [helper(g if z % 2 == 0 else 7 - g, z, 1) for z in range(LINE)] for g in range(LINE)
    ]


def from_offset(step):
    pairs = []
    for y in range(LINE):
        for z in range(LINE):
            pairs.append((helper(y, (z + step) % LINE, 0), helper(y, z, 0)))
            pairs.append((helper((y + step) % LINE, z, 1), helper(y, z, 1)))
    return pairs


def place():
    me = lax.axis_index("helper")
    return lax.div(me, 16), lax.rem(lax.div(me, 2), 8), lax.rem(me, 2)


def dot(a, b, dims=(((1,), (0,)), ((), ()))):
    return lax.dot_general(a, b, dims, preferred_element_type=F32)


def spread_kernel(held_ref, out_ref, window):
    for j in range(NB):
        window[SR * j : SR * (j + 1), :] = held_ref[16:, BS * j : BS * (j + 1)].astype(F32)[:SR]
    leading = window[...].astype(BF16).reshape(SR, 16, BS)
    for d in range(LINE):
        for j in range(NB - 1):
            out_ref[d, j] = held_ref[:16, BS * j : BS * (j + 1)]
        out_ref[d, NB - 1 :] = leading


def spread_call(held):
    vmem = pl.BlockSpec(memory_space=pltpu.VMEM)
    return pl.pallas_call(
        spread_kernel,
        out_shape=jax.ShapeDtypeStruct((LINE, SENT, 16, BS), BF16),
        in_specs=[vmem],
        out_specs=vmem,
        scratch_shapes=[pltpu.VMEM((SR * NB, BS), F32)],
        compiler_params=pltpu.CompilerParams(vmem_limit_bytes=8 * 1024 * 1024),
        name="spread",
    )(held)


def pack_kernel(line_ref, out_ref, window):
    y, z, core = place()
    label = jnp.where(lax.rem(z, 2) == 0, y, 7 - y)
    low = jnp.minimum(label, 7 - label)
    for p in range(PAIRS):
        upper = jnp.where(core == 0, jnp.where(z >= 4, 1, 0), 1 if p >= 2 else 0)
        first = jnp.where(core == 0, p, low)
        count = 14 - 2 * first + upper
        swap = jnp.where(label <= 3, 0, 1)
        large = jnp.where(core == 0, 7 - p, 2 * p + 1 - swap)
        small = jnp.where(core == 0, p, 2 * p + swap)
        for s in range(NB):
            member = jnp.where(s < count, large, small)
            piece = jnp.where(s < count, s, s - count)
            out_ref[NB * p + s] = line_ref[member, piece]
    for d in range(LINE):
        leading = line_ref[d, NB - 1 :].astype(F32)
        for j in range(NB):
            window[j, SR * d : SR * (d + 1), :] = leading[j // 4, SR * (j % 4) : SR * (j % 4 + 1), :]
    out_ref[PAIRS * NB :] = window[...].astype(BF16).reshape(2 * NB, 16, BS)


def pack_call(line):
    vmem = pl.BlockSpec(memory_space=pltpu.VMEM)
    return pl.pallas_call(
        pack_kernel,
        out_shape=jax.ShapeDtypeStruct((PIECES, 16, BS), BF16),
        in_specs=[vmem],
        out_specs=vmem,
        scratch_shapes=[pltpu.VMEM((NB, SR * LINE, BS), F32)],
        compiler_params=pltpu.CompilerParams(vmem_limit_bytes=8 * 1024 * 1024),
        name="pack",
    )(line)


def held_at(step):
    place_of = jnp.int32(0)
    for q, offset in enumerate(FROM):
        place_of = jnp.where(step == (offset + LINE) % LINE, q, place_of)
    return PIECES * place_of


def put_tiles(first, second, y, z, lt, xw):
    for core, source in ((0, first), (1, second)):
        for member in range(LINE):
            if core == 0:
                base = held_at(lax.rem(member - z + LINE, LINE))
            else:
                at = jnp.where(lax.rem(z, 2) == 0, member, 7 - member)
                base = held_at(lax.rem(at - y + LINE, LINE))
            xw[core * LINE + member] = source[pl.ds(base + PAIRS * NB, 2 * NB)]
            for p in range(PAIRS):
                if core == 0:
                    low, upper = p, member // 4
                    large, small = helper(7 - p, member, 0), helper(p, member, 0)
                else:
                    low, upper = min(member, 7 - member), p // 2
                    z_large = 2 * p + 1 if member <= 3 else 2 * p
                    large, small = helper(7 - low, z_large, 1), helper(low, 4 * p + 1 - z_large, 1)
                count = 14 - 2 * low + upper
                lt[:count, large] = source[pl.ds(base + NB * p, count)]
                rest = 2 * low + upper
                if rest:
                    lt[:rest, small] = source[pl.ds(base + NB * p + count, rest)]


def prepare_kernel(count_ref, slot_ref, block_ref, held_ref, order_ref, chosen_ref, local_ref):
    live_count = UNIT * count_ref[0]
    held = lax.broadcasted_iota(jnp.int32, (1, SLAB), 1)
    group = lax.shift_right_logical(held, 5) & 7
    turn = lax.shift_right_logical(held, 2) & 7
    first_half = held < SLAB // 2
    held_y = jnp.where(first_half, turn, jnp.where((turn & 1) == 0, group, 7 - group))
    held_z = jnp.where(first_half, group, turn)
    column = 64 * held_y + 8 * held_z + jnp.where(first_half, 0, 4) + (held & 3)
    order = jnp.where(
        lax.broadcasted_iota(jnp.int32, (SLAB, SLAB), 0) == column, 1.0, 0.0
    ).astype(BF16)

    slot = slot_ref[...]
    owner_row = jnp.broadcast_to(lax.shift_right_logical(slot, 7).astype(F32), (ROWS, ROWS))
    owner_col = owner_row.T
    local_row = jnp.broadcast_to((slot & 127).astype(F32) + 1.0, (BS, ROWS))
    local_ref[...] = local_row.T.astype(BF16)
    i0 = lax.broadcasted_iota(jnp.int32, (ROWS, ROWS), 0)
    i1 = lax.broadcasted_iota(jnp.int32, (ROWS, ROWS), 1)
    earlier = jnp.where((owner_row == owner_col) & (i0 < i1) & (i0 < live_count), 1.0, 0.0)
    rank = jnp.sum(earlier, axis=0, keepdims=True)
    target = owner_row * CAP + rank
    chosen_ref[...] = jnp.where((target == i0.astype(F32)) & (i1 < live_count), 1.0, 0.0).astype(BF16)
    held_ref[...] = dot(block_ref[...], order)
    order_ref[...] = order


def prepare_call(count, slot, block):
    vmem = pl.BlockSpec(memory_space=pltpu.VMEM)
    return pl.pallas_call(
        prepare_kernel,
        out_shape=(
            jax.ShapeDtypeStruct((ROWS, SLAB), F32),
            jax.ShapeDtypeStruct((SLAB, SLAB), BF16),
            jax.ShapeDtypeStruct((SLOTS, ROWS), BF16),
            jax.ShapeDtypeStruct((ROWS, BS), BF16),
        ),
        in_specs=[pl.BlockSpec(memory_space=pltpu.SMEM), vmem, vmem],
        out_specs=(vmem,) * 4,
        compiler_params=pltpu.CompilerParams(vmem_limit_bytes=8 * 1024 * 1024),
        cost_estimate=pl.CostEstimate(flops=2 * ROWS * SLAB * SLAB, bytes_accessed=1 << 20, transcendentals=0),
        name="prepare",
    )(count, slot, block)


def front_kernel(
    count_ref, mine_ref, other_ref, rows_ref, inv_ref, block_ref, order_ref, chosen_ref, local_ref,
    factor_ref, send_ref, lt, xw, solved, wfac,
):
    y, z, core = place()

    @pl.when(core == 0)
    def _():
        put_tiles(mine_ref, other_ref, y, z, lt, xw)

    @pl.when(core == 1)
    def _():
        put_tiles(other_ref, mine_ref, y, z, lt, xw)

    live_count = UNIT * count_ref[0]
    live = lax.broadcasted_iota(jnp.int32, (ROWS, 1), 0) < live_count

    def window_piece(k):
        return xw[:, 2 * k : 2 * k + 2].reshape(SLAB, BS)

    def panel_piece(j, top, count):
        return lt[j, top // 16 : (top + count) // 16].reshape(count, BS)

    def start_block(k):
        return jnp.concatenate([window_piece(k), rows_ref[:, BS * k : BS * (k + 1)]], axis=0).astype(F32)

    def scale(part, k):
        f = dot(part, inv_ref[k]).astype(BF16)
        wfac[:, BS * k : BS * (k + 1)] = f[:SLAB]
        factor_ref[:, BS * k : BS * (k + 1)] = jnp.where(live, f[SLAB:], jnp.zeros((), BF16))

    def pair(s):
        return jnp.concatenate([start_block(2 * s), start_block(2 * s + 1)], axis=1)

    pending = pair(0)
    last = None
    for s in range(NB // 2):
        lo = 256 * s
        k0, k1 = 2 * s, 2 * s + 1
        x = pending
        if s > 0:
            panel = jnp.concatenate([panel_piece(j, lo, 256) for j in (k0 - 2, k0 - 1)], axis=1)
            x = x - dot(last, panel, NT)
        s0 = x[:, :BS].astype(BF16)
        if s + 1 < NB // 2:
            pending = pair(s + 1)
            if s > 0:
                panel = jnp.concatenate([panel_piece(j, lo + 256, 256) for j in range(k0)], axis=1)
                pending = pending - dot(solved[:, :lo], panel, NT)
        s1 = (x[:, BS:] - dot(s0, panel_piece(k0, lo + BS, BS), NT)).astype(BF16)
        last = jnp.concatenate([s0, s1], axis=1)
        solved[:, lo : lo + 256] = last
        scale(s0, k0)
        scale(s1, k1)

    product = dot(solved[SLAB:, :], wfac[...], NT)
    held_contribution = (block_ref[...] - product).astype(BF16)
    contribution = dot(held_contribution, order_ref[...], NT).astype(BF16)

    payload = jnp.concatenate([contribution, local_ref[...]], axis=1)
    send_ref[...] = dot(chosen_ref[...], payload).astype(BF16)


def front_call(mine, other, rows, inverse, count, prepared):
    vmem = pl.BlockSpec(memory_space=pltpu.VMEM)
    return pl.pallas_call(
        front_kernel,
        out_shape=(
            jax.ShapeDtypeStruct((ROWS, NPIV), BF16),
            jax.ShapeDtypeStruct((SLOTS, WIDE), BF16),
        ),
        in_specs=[pl.BlockSpec(memory_space=pltpu.SMEM)] + [vmem] * 8,
        out_specs=(vmem, vmem),
        scratch_shapes=[
            pltpu.VMEM((NB, HELPERS, 16, BS), BF16),
            pltpu.VMEM((2 * LINE, 2 * NB, 16, BS), BF16),
            pltpu.VMEM((ALL, NPIV), BF16),
            pltpu.VMEM((SLAB, NPIV), BF16),
        ],
        compiler_params=pltpu.CompilerParams(vmem_limit_bytes=32 * 1024 * 1024),
        name="front",
    )(count, mine, other, rows, inverse, *prepared)


def assemble_kernel(got_ref, out_ref):
    got = got_ref[...]
    local = got[:, SLAB:].astype(F32)
    wanted = lax.broadcasted_iota(jnp.int32, (SLOTS, PROWS), 1).astype(F32) + 1.0
    chooser = jnp.where(local == wanted, 1.0, 0.0).astype(BF16)
    out_ref[...] = dot(chooser, got[:, :SLAB], TN)


def assemble_call(got):
    vmem = pl.BlockSpec(memory_space=pltpu.VMEM)
    return pl.pallas_call(
        assemble_kernel,
        out_shape=jax.ShapeDtypeStruct((PROWS, SLAB), F32),
        in_specs=[vmem],
        out_specs=vmem,
        compiler_params=pltpu.CompilerParams(vmem_limit_bytes=8 * 1024 * 1024),
        name="assemble",
    )(got)


def per_device(lower_panel, pivot_inverse, lower_rows, window_block, block_count, parent_slot):
    def receive(block, step):
        return lax.ppermute(block, "helper", from_offset(step))

    line = lax.all_to_all(
        spread_call(jnp.concatenate([lower_panel, lower_rows[:16]])), "helper", 0, 0, tiled=True, axis_index_groups=line_groups()
    )
    own = pack_call(line)
    half = PIECES // 2
    up, down = receive(own, 1), receive(own, -1)
    up2, down2 = receive(own, 2), receive(own, -2)
    mine = jnp.concatenate(
        [own, up, down, up2, down2]
        + [receive(up2, 1), receive(down2, -1), receive(up2[:half], 2), receive(down2[half:], -2)]
    )
    other = lax.ppermute(mine, "helper", [(h, h ^ 1) for h in range(HELPERS)])
    factor, send = front_call(
        mine, other, lower_rows, pivot_inverse, block_count,
        prepare_call(block_count, parent_slot.reshape(1, ROWS), window_block),
    )
    got = lax.all_to_all(
        send.reshape(HELPERS, CAP, WIDE), "helper", split_axis=0, concat_axis=0, tiled=True
    )
    return factor, assemble_call(got.reshape(SLOTS, WIDE))


def solution(mesh):
    return jax.shard_map(
        per_device,
        mesh=mesh,
        in_specs=(
            P(("front", "helper"), None),
            P("front", None, None),
            P(("front", "helper"), None),
            P(("front", "helper"), None),
            P(("front", "helper")),
            P(("front", "helper")),
        ),
        out_specs=(P(("front", "helper"), None), P(("front", "helper"), None)),
        check_vma=False,
    )
```

```python
import functools

import jax
import jax.numpy as jnp
from jax import lax
from jax.experimental import pallas as pl
from jax.experimental.pallas import tpu as pltpu
from jax.sharding import PartitionSpec as P

UNIT = 128
SR = 4
PROWS = 128
BS = 128
NB = 16
NPIV = 2048
ROWS = 256
SLAB = 512
HELPERS = 128
CAP = 2
SLOTS = HELPERS * CAP
WIDE = SLAB + 128
ALL = SLAB + ROWS
F32 = jnp.float32
BF16 = jnp.bfloat16
NT = (((1,), (1,)), ((), ()))
TN = (((0,), (0,)), ((), ()))
LINE = 8
PAIRS = 4
SENT = NB - 1 + SR
PIECES = PAIRS * NB + 2 * NB
FROM = (0, 1, -1, 2, -2, 3, -3, 4)


def helper(y, z, core):
    return 2 * LINE * y + 2 * z + core


def line_groups():
    return [[helper(y, z, 0) for y in range(LINE)] for z in range(LINE)] + [
        [helper(g if z % 2 == 0 else 7 - g, z, 1) for z in range(LINE)] for g in range(LINE)
    ]


def from_offset(step):
    pairs = []
    for y in range(LINE):
        for z in range(LINE):
            pairs.append((helper(y, (z + step) % LINE, 0), helper(y, z, 0)))
            pairs.append((helper((y + step) % LINE, z, 1), helper(y, z, 1)))
    return pairs


def place():
    me = lax.axis_index("helper")
    return lax.div(me, 16), lax.rem(lax.div(me, 2), 8), lax.rem(me, 2)


def dot(a, b, dims=(((1,), (0,)), ((), ()))):
    return lax.dot_general(a, b, dims, preferred_element_type=F32)


def spread_kernel(held_ref, out_ref, window):
    for j in range(NB):
        window[SR * j : SR * (j + 1), :] = held_ref[16:, BS * j : BS * (j + 1)].astype(F32)[:SR]
    leading = window[...].astype(BF16).reshape(SR, 16, BS)
    for d in range(LINE):
        for j in range(NB - 1):
            out_ref[d, j] = held_ref[:16, BS * j : BS * (j + 1)]
        out_ref[d, NB - 1 :] = leading


def spread_call(held):
    vmem = pl.BlockSpec(memory_space=pltpu.VMEM)
    return pl.pallas_call(
        spread_kernel,
        out_shape=jax.ShapeDtypeStruct((LINE, SENT, 16, BS), BF16),
        in_specs=[vmem],
        out_specs=vmem,
        scratch_shapes=[pltpu.VMEM((SR * NB, BS), F32)],
        compiler_params=pltpu.CompilerParams(vmem_limit_bytes=8 * 1024 * 1024),
        name="spread",
    )(held)


def pack_kernel(line_ref, out_ref, window):
    y, z, core = place()
    label = jnp.where(lax.rem(z, 2) == 0, y, 7 - y)
    low = jnp.minimum(label, 7 - label)
    for p in range(PAIRS):
        upper = jnp.where(core == 0, jnp.where(z >= 4, 1, 0), 1 if p >= 2 else 0)
        first = jnp.where(core == 0, p, low)
        count = 14 - 2 * first + upper
        swap = jnp.where(label <= 3, 0, 1)
        large = jnp.where(core == 0, 7 - p, 2 * p + 1 - swap)
        small = jnp.where(core == 0, p, 2 * p + swap)
        for s in range(NB):
            member = jnp.where(s < count, large, small)
            piece = jnp.where(s < count, s, s - count)
            out_ref[NB * p + s] = line_ref[member, piece]
    for d in range(LINE):
        leading = line_ref[d, NB - 1 :].astype(F32)
        for j in range(NB):
            window[j, SR * d : SR * (d + 1), :] = leading[j // 4, SR * (j % 4) : SR * (j % 4 + 1), :]
    out_ref[PAIRS * NB :] = window[...].astype(BF16).reshape(2 * NB, 16, BS)


def pack_call(line):
    vmem = pl.BlockSpec(memory_space=pltpu.VMEM)
    return pl.pallas_call(
        pack_kernel,
        out_shape=jax.ShapeDtypeStruct((PIECES, 16, BS), BF16),
        in_specs=[vmem],
        out_specs=vmem,
        scratch_shapes=[pltpu.VMEM((NB, SR * LINE, BS), F32)],
        compiler_params=pltpu.CompilerParams(vmem_limit_bytes=8 * 1024 * 1024),
        name="pack",
    )(line)


def held_at(step):
    place_of = jnp.int32(0)
    for q, offset in enumerate(FROM):
        place_of = jnp.where(step == (offset + LINE) % LINE, q, place_of)
    return PIECES * place_of


def put_tiles(first, second, y, z, lt, xw):
    for core, source in ((0, first), (1, second)):
        for member in range(LINE):
            if core == 0:
                base = held_at(lax.rem(member - z + LINE, LINE))
            else:
                at = jnp.where(lax.rem(z, 2) == 0, member, 7 - member)
                base = held_at(lax.rem(at - y + LINE, LINE))
            xw[core * LINE + member] = source[pl.ds(base + PAIRS * NB, 2 * NB)]
            for p in range(PAIRS):
                if core == 0:
                    low, upper = p, member // 4
                    large, small = helper(7 - p, member, 0), helper(p, member, 0)
                else:
                    low, upper = min(member, 7 - member), p // 2
                    z_large = 2 * p + 1 if member <= 3 else 2 * p
                    large, small = helper(7 - low, z_large, 1), helper(low, 4 * p + 1 - z_large, 1)
                count = 14 - 2 * low + upper
                lt[:count, large] = source[pl.ds(base + NB * p, count)]
                rest = 2 * low + upper
                if rest:
                    lt[:rest, small] = source[pl.ds(base + NB * p + count, rest)]


def prepare_kernel(count_ref, slot_ref, block_ref, held_ref, order_ref, chosen_ref, local_ref):
    live_count = UNIT * count_ref[0]
    held = lax.broadcasted_iota(jnp.int32, (1, SLAB), 1)
    group = lax.shift_right_logical(held, 5) & 7
    turn = lax.shift_right_logical(held, 2) & 7
    first_half = held < SLAB // 2
    held_y = jnp.where(first_half, turn, jnp.where((turn & 1) == 0, group, 7 - group))
    held_z = jnp.where(first_half, group, turn)
    column = 64 * held_y + 8 * held_z + jnp.where(first_half, 0, 4) + (held & 3)
    order = jnp.where(
        lax.broadcasted_iota(jnp.int32, (SLAB, SLAB), 0) == column, 1.0, 0.0
    ).astype(BF16)

    slot = slot_ref[...]
    owner_row = jnp.broadcast_to(lax.shift_right_logical(slot, 7).astype(F32), (ROWS, ROWS))
    owner_col = owner_row.T
    local_row = jnp.broadcast_to((slot & 127).astype(F32) + 1.0, (BS, ROWS))
    local_ref[...] = local_row.T.astype(BF16)
    i0 = lax.broadcasted_iota(jnp.int32, (ROWS, ROWS), 0)
    i1 = lax.broadcasted_iota(jnp.int32, (ROWS, ROWS), 1)
    earlier = jnp.where((owner_row == owner_col) & (i0 < i1) & (i0 < live_count), 1.0, 0.0)
    rank = jnp.sum(earlier, axis=0, keepdims=True)
    target = owner_row * CAP + rank
    chosen_ref[...] = jnp.where((target == i0.astype(F32)) & (i1 < live_count), 1.0, 0.0).astype(BF16)
    held_ref[...] = dot(block_ref[...], order)
    order_ref[...] = order


def prepare_call(count, slot, block):
    vmem = pl.BlockSpec(memory_space=pltpu.VMEM)
    return pl.pallas_call(
        prepare_kernel,
        out_shape=(
            jax.ShapeDtypeStruct((ROWS, SLAB), F32),
            jax.ShapeDtypeStruct((SLAB, SLAB), BF16),
            jax.ShapeDtypeStruct((SLOTS, ROWS), BF16),
            jax.ShapeDtypeStruct((ROWS, BS), BF16),
        ),
        in_specs=[pl.BlockSpec(memory_space=pltpu.SMEM), vmem, vmem],
        out_specs=(vmem,) * 4,
        compiler_params=pltpu.CompilerParams(vmem_limit_bytes=8 * 1024 * 1024),
        cost_estimate=pl.CostEstimate(flops=2 * ROWS * SLAB * SLAB, bytes_accessed=1 << 20, transcendentals=0),
        name="prepare",
    )(count, slot, block)


def front_kernel(
    count_ref, mine_ref, other_ref, rows_ref, inv_ref, block_ref, order_ref, chosen_ref, local_ref,
    factor_ref, send_ref, lt, xw, solved, wfac,
):
    y, z, core = place()

    @pl.when(core == 0)
    def _():
        put_tiles(mine_ref, other_ref, y, z, lt, xw)

    @pl.when(core == 1)
    def _():
        put_tiles(other_ref, mine_ref, y, z, lt, xw)

    live_count = UNIT * count_ref[0]
    live = lax.broadcasted_iota(jnp.int32, (ROWS, 1), 0) < live_count

    def window_piece(k):
        return xw[:, 2 * k : 2 * k + 2].reshape(SLAB, BS)

    def panel_piece(j, top, count):
        return lt[j, top // 16 : (top + count) // 16].reshape(count, BS)

    def start_block(k):
        return jnp.concatenate([window_piece(k), rows_ref[:, BS * k : BS * (k + 1)]], axis=0).astype(F32)

    def scale(part, k):
        f = dot(part, inv_ref[k]).astype(BF16)
        wfac[:, BS * k : BS * (k + 1)] = f[:SLAB]
        factor_ref[:, BS * k : BS * (k + 1)] = jnp.where(live, f[SLAB:], jnp.zeros((), BF16))

    def pair(s):
        return jnp.concatenate([start_block(2 * s), start_block(2 * s + 1)], axis=1)

    groups = ((0, 512), (512, 768))

    def start_rows(k, g):
        r0, r1 = groups[g]
        parts = []
        if r0 < SLAB:
            parts.append(window_piece(k)[r0 : min(r1, SLAB)])
        if r1 > SLAB:
            parts.append(rows_ref[max(r0, SLAB) - SLAB : r1 - SLAB, BS * k : BS * (k + 1)])
        return jnp.concatenate(parts, axis=0).astype(F32)

    def pair2(s, g):
        return jnp.concatenate([start_rows(2 * s, g), start_rows(2 * s + 1, g)], axis=1)

    pend = [pair2(0, g) for g in range(len(groups))]
    lasts = [None] * len(groups)
    for s in range(NB // 2):
        lo = 256 * s
        k0, k1 = 2 * s, 2 * s + 1
        xs = list(pend)
        if s > 0:
            panel = jnp.concatenate([panel_piece(j, lo, 256) for j in (k0 - 2, k0 - 1)], axis=1)
            xs = [xs[g] - dot(lasts[g], panel, NT) for g in range(len(groups))]
        s0s = [x[:, :BS].astype(BF16) for x in xs]
        if s + 1 < NB // 2:
            pend = [pair2(s + 1, g) for g in range(len(groups))]
            if s > 0:
                panel = jnp.concatenate([panel_piece(j, lo + 256, 256) for j in range(k0)], axis=1)
                pend = [pend[g] - dot(solved[r0:r1, :lo], panel, NT) for g, (r0, r1) in enumerate(groups)]
        diag = panel_piece(k0, lo + BS, BS)
        s1s = [(xs[g][:, BS:] - dot(s0s[g], diag, NT)).astype(BF16) for g in range(len(groups))]
        lasts = [jnp.concatenate([s0s[g], s1s[g]], axis=1) for g in range(len(groups))]
        for g, (r0, r1) in enumerate(groups):
            solved[r0:r1, lo : lo + 256] = lasts[g]
        scale(jnp.concatenate(s0s, axis=0), k0)
        scale(jnp.concatenate(s1s, axis=0), k1)

    product = dot(solved[SLAB:, :], wfac[...], NT)
    held_contribution = (block_ref[...] - product).astype(BF16)
    contribution = dot(held_contribution, order_ref[...], NT).astype(BF16)

    payload = jnp.concatenate([contribution, local_ref[...]], axis=1)
    send_ref[...] = dot(chosen_ref[...], payload).astype(BF16)


def front_call(mine, other, rows, inverse, count, prepared):
    vmem = pl.BlockSpec(memory_space=pltpu.VMEM)
    return pl.pallas_call(
        front_kernel,
        out_shape=(
            jax.ShapeDtypeStruct((ROWS, NPIV), BF16),
            jax.ShapeDtypeStruct((SLOTS, WIDE), BF16),
        ),
        in_specs=[pl.BlockSpec(memory_space=pltpu.SMEM)] + [vmem] * 8,
        out_specs=(vmem, vmem),
        scratch_shapes=[
            pltpu.VMEM((NB, HELPERS, 16, BS), BF16),
            pltpu.VMEM((2 * LINE, 2 * NB, 16, BS), BF16),
            pltpu.VMEM((ALL, NPIV), BF16),
            pltpu.VMEM((SLAB, NPIV), BF16),
        ],
        compiler_params=pltpu.CompilerParams(vmem_limit_bytes=32 * 1024 * 1024),
        name="front",
    )(count, mine, other, rows, inverse, *prepared)


def assemble_kernel(got_ref, out_ref):
    got = got_ref[...]
    local = got[:, SLAB:].astype(F32)
    wanted = lax.broadcasted_iota(jnp.int32, (SLOTS, PROWS), 1).astype(F32) + 1.0
    chooser = jnp.where(local == wanted, 1.0, 0.0).astype(BF16)
    out_ref[...] = dot(chooser, got[:, :SLAB], TN)


def assemble_call(got):
    vmem = pl.BlockSpec(memory_space=pltpu.VMEM)
    return pl.pallas_call(
        assemble_kernel,
        out_shape=jax.ShapeDtypeStruct((PROWS, SLAB), F32),
        in_specs=[vmem],
        out_specs=vmem,
        compiler_params=pltpu.CompilerParams(vmem_limit_bytes=8 * 1024 * 1024),
        name="assemble",
    )(got)


def per_device(lower_panel, pivot_inverse, lower_rows, window_block, block_count, parent_slot):
    def receive(block, step):
        return lax.ppermute(block, "helper", from_offset(step))

    line = lax.all_to_all(
        spread_call(jnp.concatenate([lower_panel, lower_rows[:16]])), "helper", 0, 0, tiled=True, axis_index_groups=line_groups()
    )
    own = pack_call(line)
    half = PIECES // 2
    up, down = receive(own, 1), receive(own, -1)
    up2, down2 = receive(own, 2), receive(own, -2)
    mine = jnp.concatenate(
        [own, up, down, up2, down2]
        + [receive(up2, 1), receive(down2, -1), receive(up2[:half], 2), receive(down2[half:], -2)]
    )
    other = lax.ppermute(mine, "helper", [(h, h ^ 1) for h in range(HELPERS)])
    factor, send = front_call(
        mine, other, lower_rows, pivot_inverse, block_count,
        prepare_call(block_count, parent_slot.reshape(1, ROWS), window_block),
    )
    got = lax.all_to_all(
        send.reshape(HELPERS, CAP, WIDE), "helper", split_axis=0, concat_axis=0, tiled=True
    )
    return factor, assemble_call(got.reshape(SLOTS, WIDE))


def solution(mesh):
    return jax.shard_map(
        per_device,
        mesh=mesh,
        in_specs=(
            P(("front", "helper"), None),
            P("front", None, None),
            P(("front", "helper"), None),
            P(("front", "helper"), None),
            P(("front", "helper")),
            P(("front", "helper")),
        ),
        out_specs=(P(("front", "helper"), None), P(("front", "helper"), None)),
        check_vma=False,
    )
```

```python
import functools

import jax
import jax.numpy as jnp
from jax import lax
from jax.experimental import pallas as pl
from jax.experimental.pallas import tpu as pltpu
from jax.sharding import PartitionSpec as P

UNIT = 128
SR = 4
PROWS = 128
BS = 128
NB = 16
NPIV = 2048
ROWS = 256
SLAB = 512
HELPERS = 128
CAP = 2
SLOTS = HELPERS * CAP
WIDE = SLAB + 128
ALL = SLAB + ROWS
F32 = jnp.float32
BF16 = jnp.bfloat16
NT = (((1,), (1,)), ((), ()))
TN = (((0,), (0,)), ((), ()))
LINE = 8
PAIRS = 4
SENT = NB - 1 + SR
PIECES = PAIRS * NB + 2 * NB
FROM = (0, 1, -1, 2, -2, 3, -3, 4)


def helper(y, z, core):
    return 2 * LINE * y + 2 * z + core


def line_groups():
    return [[helper(y, z, 0) for y in range(LINE)] for z in range(LINE)] + [
        [helper(g if z % 2 == 0 else 7 - g, z, 1) for z in range(LINE)] for g in range(LINE)
    ]


def from_offset(step):
    pairs = []
    for y in range(LINE):
        for z in range(LINE):
            pairs.append((helper(y, (z + step) % LINE, 0), helper(y, z, 0)))
            pairs.append((helper((y + step) % LINE, z, 1), helper(y, z, 1)))
    return pairs


def place():
    me = lax.axis_index("helper")
    return lax.div(me, 16), lax.rem(lax.div(me, 2), 8), lax.rem(me, 2)


def dot(a, b, dims=(((1,), (0,)), ((), ()))):
    return lax.dot_general(a, b, dims, preferred_element_type=F32)


def spread_kernel(held_ref, out_ref, window):
    for j in range(NB):
        window[SR * j : SR * (j + 1), :] = held_ref[16:, BS * j : BS * (j + 1)].astype(F32)[:SR]
    leading = window[...].astype(BF16).reshape(SR, 16, BS)
    for d in range(LINE):
        for j in range(NB - 1):
            out_ref[d, j] = held_ref[:16, BS * j : BS * (j + 1)]
        out_ref[d, NB - 1 :] = leading


def spread_call(held):
    vmem = pl.BlockSpec(memory_space=pltpu.VMEM)
    return pl.pallas_call(
        spread_kernel,
        out_shape=jax.ShapeDtypeStruct((LINE, SENT, 16, BS), BF16),
        in_specs=[vmem],
        out_specs=vmem,
        scratch_shapes=[pltpu.VMEM((SR * NB, BS), F32)],
        compiler_params=pltpu.CompilerParams(vmem_limit_bytes=8 * 1024 * 1024),
        name="spread",
    )(held)


def pack_kernel(line_ref, out_ref, window):
    y, z, core = place()
    label = jnp.where(lax.rem(z, 2) == 0, y, 7 - y)
    low = jnp.minimum(label, 7 - label)
    for p in range(PAIRS):
        upper = jnp.where(core == 0, jnp.where(z >= 4, 1, 0), 1 if p >= 2 else 0)
        first = jnp.where(core == 0, p, low)
        count = 14 - 2 * first + upper
        swap = jnp.where(label <= 3, 0, 1)
        large = jnp.where(core == 0, 7 - p, 2 * p + 1 - swap)
        small = jnp.where(core == 0, p, 2 * p + swap)
        for s in range(NB):
            member = jnp.where(s < count, large, small)
            piece = jnp.where(s < count, s, s - count)
            out_ref[NB * p + s] = line_ref[member, piece]
    for d in range(LINE):
        leading = line_ref[d, NB - 1 :].astype(F32)
        for j in range(NB):
            window[j, SR * d : SR * (d + 1), :] = leading[j // 4, SR * (j % 4) : SR * (j % 4 + 1), :]
    out_ref[PAIRS * NB :] = window[...].astype(BF16).reshape(2 * NB, 16, BS)


def pack_call(line):
    vmem = pl.BlockSpec(memory_space=pltpu.VMEM)
    return pl.pallas_call(
        pack_kernel,
        out_shape=jax.ShapeDtypeStruct((PIECES, 16, BS), BF16),
        in_specs=[vmem],
        out_specs=vmem,
        scratch_shapes=[pltpu.VMEM((NB, SR * LINE, BS), F32)],
        compiler_params=pltpu.CompilerParams(vmem_limit_bytes=8 * 1024 * 1024),
        name="pack",
    )(line)


def held_at(step):
    place_of = jnp.int32(0)
    for q, offset in enumerate(FROM):
        place_of = jnp.where(step == (offset + LINE) % LINE, q, place_of)
    return PIECES * place_of


def put_tiles(first, second, y, z, lt, xw):
    for core, source in ((0, first), (1, second)):
        for member in range(LINE):
            if core == 0:
                base = held_at(lax.rem(member - z + LINE, LINE))
            else:
                at = jnp.where(lax.rem(z, 2) == 0, member, 7 - member)
                base = held_at(lax.rem(at - y + LINE, LINE))
            xw[core * LINE + member] = source[pl.ds(base + PAIRS * NB, 2 * NB)]
            for p in range(PAIRS):
                if core == 0:
                    low, upper = p, member // 4
                    large, small = helper(7 - p, member, 0), helper(p, member, 0)
                else:
                    low, upper = min(member, 7 - member), p // 2
                    z_large = 2 * p + 1 if member <= 3 else 2 * p
                    large, small = helper(7 - low, z_large, 1), helper(low, 4 * p + 1 - z_large, 1)
                count = 14 - 2 * low + upper
                lt[:count, large] = source[pl.ds(base + NB * p, count)]
                rest = 2 * low + upper
                if rest:
                    lt[:rest, small] = source[pl.ds(base + NB * p + count, rest)]


def prepare_kernel(count_ref, slot_ref, block_ref, held_ref, order_ref, chosen_ref, local_ref):
    live_count = UNIT * count_ref[0]
    held = lax.broadcasted_iota(jnp.int32, (1, SLAB), 1)
    group = lax.shift_right_logical(held, 5) & 7
    turn = lax.shift_right_logical(held, 2) & 7
    first_half = held < SLAB // 2
    held_y = jnp.where(first_half, turn, jnp.where((turn & 1) == 0, group, 7 - group))
    held_z = jnp.where(first_half, group, turn)
    column = 64 * held_y + 8 * held_z + jnp.where(first_half, 0, 4) + (held & 3)
    order = jnp.where(
        lax.broadcasted_iota(jnp.int32, (SLAB, SLAB), 0) == column, 1.0, 0.0
    ).astype(BF16)

    slot = slot_ref[...]
    owner_row = jnp.broadcast_to(lax.shift_right_logical(slot, 7).astype(F32), (ROWS, ROWS))
    owner_col = owner_row.T
    local_row = jnp.broadcast_to((slot & 127).astype(F32) + 1.0, (BS, ROWS))
    local_ref[...] = local_row.T.astype(BF16)
    i0 = lax.broadcasted_iota(jnp.int32, (ROWS, ROWS), 0)
    i1 = lax.broadcasted_iota(jnp.int32, (ROWS, ROWS), 1)
    earlier = jnp.where((owner_row == owner_col) & (i0 < i1) & (i0 < live_count), 1.0, 0.0)
    rank = jnp.sum(earlier, axis=0, keepdims=True)
    target = owner_row * CAP + rank
    chosen_ref[...] = jnp.where((target == i0.astype(F32)) & (i1 < live_count), 1.0, 0.0).astype(BF16)
    held_ref[...] = dot(block_ref[...], order)
    order_ref[...] = order


def prepare_call(count, slot, block):
    vmem = pl.BlockSpec(memory_space=pltpu.VMEM)
    return pl.pallas_call(
        prepare_kernel,
        out_shape=(
            jax.ShapeDtypeStruct((ROWS, SLAB), F32),
            jax.ShapeDtypeStruct((SLAB, SLAB), BF16),
            jax.ShapeDtypeStruct((SLOTS, ROWS), BF16),
            jax.ShapeDtypeStruct((ROWS, BS), BF16),
        ),
        in_specs=[pl.BlockSpec(memory_space=pltpu.SMEM), vmem, vmem],
        out_specs=(vmem,) * 4,
        compiler_params=pltpu.CompilerParams(vmem_limit_bytes=8 * 1024 * 1024),
        cost_estimate=pl.CostEstimate(flops=2 * ROWS * SLAB * SLAB, bytes_accessed=1 << 20, transcendentals=0),
        name="prepare",
    )(count, slot, block)


def front_kernel(
    count_ref, mine_ref, other_ref, rows_ref, inv_ref, block_ref, order_ref, chosen_ref, local_ref,
    factor_ref, send_ref, lt, xw, solved, wfac,
):
    y, z, core = place()

    @pl.when(core == 0)
    def _():
        put_tiles(mine_ref, other_ref, y, z, lt, xw)

    @pl.when(core == 1)
    def _():
        put_tiles(other_ref, mine_ref, y, z, lt, xw)

    live_count = UNIT * count_ref[0]
    live = lax.broadcasted_iota(jnp.int32, (ROWS, 1), 0) < live_count

    def window_piece(k):
        return xw[:, 2 * k : 2 * k + 2].reshape(SLAB, BS)

    def panel_piece(j, top, count):
        return lt[j, top // 16 : (top + count) // 16].reshape(count, BS)

    def start_block(k):
        return jnp.concatenate([window_piece(k), rows_ref[:, BS * k : BS * (k + 1)]], axis=0).astype(F32)

    def scale(part, k):
        f = dot(part, inv_ref[k]).astype(BF16)
        wfac[:, BS * k : BS * (k + 1)] = f[:SLAB]
        factor_ref[:, BS * k : BS * (k + 1)] = jnp.where(live, f[SLAB:], jnp.zeros((), BF16))

    def pair(s):
        return jnp.concatenate([start_block(2 * s), start_block(2 * s + 1)], axis=1)

    groups = ((0, 512), (512, 768))

    def start_rows(k, g):
        r0, r1 = groups[g]
        parts = []
        if r0 < SLAB:
            parts.append(window_piece(k)[r0 : min(r1, SLAB)])
        if r1 > SLAB:
            parts.append(rows_ref[max(r0, SLAB) - SLAB : r1 - SLAB, BS * k : BS * (k + 1)])
        return jnp.concatenate(parts, axis=0).astype(F32)

    def pair2(s, g):
        return jnp.concatenate([start_rows(2 * s, g), start_rows(2 * s + 1, g)], axis=1)

    pend = [pair2(0, g) for g in range(len(groups))]
    lasts = [None] * len(groups)
    for s in range(NB // 2):
        lo = 256 * s
        k0, k1 = 2 * s, 2 * s + 1
        xs = list(pend)
        if s > 0:
            panel = jnp.concatenate([panel_piece(j, lo, 256) for j in (k0 - 2, k0 - 1)], axis=1)
            xs = [xs[g] - dot(lasts[g], panel, NT) for g in range(len(groups))]
        s0s = [x[:, :BS].astype(BF16) for x in xs]
        if s + 1 < NB // 2:
            pend = [pair2(s + 1, g) for g in range(len(groups))]
            if s > 0:
                panel = jnp.concatenate([panel_piece(j, lo + 256, 256) for j in range(k0)], axis=1)
                pend = [pend[g] - dot(solved[r0:r1, :lo], panel, NT) for g, (r0, r1) in enumerate(groups)]
        diag = panel_piece(k0, lo + BS, BS)
        s1s = [(xs[g][:, BS:] - dot(s0s[g], diag, NT)).astype(BF16) for g in range(len(groups))]
        lasts = [jnp.concatenate([s0s[g], s1s[g]], axis=1) for g in range(len(groups))]
        for g, (r0, r1) in enumerate(groups):
            solved[r0:r1, lo : lo + 256] = lasts[g]
        scale(jnp.concatenate(s0s, axis=0), k0)
        scale(jnp.concatenate(s1s, axis=0), k1)

    product = dot(solved[SLAB:, :], wfac[...], NT)
    held_contribution = jnp.where(live, block_ref[...] - product, 0.0).astype(BF16)
    contribution = dot(held_contribution, order_ref[...], NT).astype(BF16)

    payload = jnp.concatenate([contribution, local_ref[...]], axis=1)
    send_ref[...] = dot(chosen_ref[...], payload).astype(BF16)


def front_call(mine, other, rows, inverse, count, prepared):
    vmem = pl.BlockSpec(memory_space=pltpu.VMEM)
    return pl.pallas_call(
        front_kernel,
        out_shape=(
            jax.ShapeDtypeStruct((ROWS, NPIV), BF16),
            jax.ShapeDtypeStruct((SLOTS, WIDE), BF16),
        ),
        in_specs=[pl.BlockSpec(memory_space=pltpu.SMEM)] + [vmem] * 8,
        out_specs=(vmem, vmem),
        scratch_shapes=[
            pltpu.VMEM((NB, HELPERS, 16, BS), BF16),
            pltpu.VMEM((2 * LINE, 2 * NB, 16, BS), BF16),
            pltpu.VMEM((ALL, NPIV), BF16),
            pltpu.VMEM((SLAB, NPIV), BF16),
        ],
        compiler_params=pltpu.CompilerParams(vmem_limit_bytes=32 * 1024 * 1024),
        name="front",
    )(count, mine, other, rows, inverse, *prepared)


def assemble_kernel(got_ref, out_ref):
    got = got_ref[...]
    local = got[:, SLAB:].astype(F32)
    wanted = lax.broadcasted_iota(jnp.int32, (SLOTS, PROWS), 1).astype(F32) + 1.0
    chooser = jnp.where(local == wanted, 1.0, 0.0).astype(BF16)
    out_ref[...] = dot(chooser, got[:, :SLAB], TN)


def assemble_call(got):
    vmem = pl.BlockSpec(memory_space=pltpu.VMEM)
    return pl.pallas_call(
        assemble_kernel,
        out_shape=jax.ShapeDtypeStruct((PROWS, SLAB), F32),
        in_specs=[vmem],
        out_specs=vmem,
        compiler_params=pltpu.CompilerParams(vmem_limit_bytes=8 * 1024 * 1024),
        name="assemble",
    )(got)


def per_device(lower_panel, pivot_inverse, lower_rows, window_block, block_count, parent_slot):
    def receive(block, step):
        return lax.ppermute(block, "helper", from_offset(step))

    line = lax.all_to_all(
        spread_call(jnp.concatenate([lower_panel, lower_rows[:16]])), "helper", 0, 0, tiled=True, axis_index_groups=line_groups()
    )
    own = pack_call(line)
    half = PIECES // 2
    up, down = receive(own, 1), receive(own, -1)
    up2, down2 = receive(own, 2), receive(own, -2)
    mine = jnp.concatenate(
        [own, up, down, up2, down2]
        + [receive(up2, 1), receive(down2, -1), receive(up2[:half], 2), receive(down2[half:], -2)]
    )
    other = lax.ppermute(mine, "helper", [(h, h ^ 1) for h in range(HELPERS)])
    factor, send = front_call(
        mine, other, lower_rows, pivot_inverse, block_count,
        prepare_call(block_count, parent_slot.reshape(1, ROWS), window_block),
    )
    got = lax.all_to_all(
        send.reshape(HELPERS, CAP, WIDE), "helper", split_axis=0, concat_axis=0, tiled=True
    )
    return factor, assemble_call(got.reshape(SLOTS, WIDE))


def solution(mesh):
    return jax.shard_map(
        per_device,
        mesh=mesh,
        in_specs=(
            P(("front", "helper"), None),
            P("front", None, None),
            P(("front", "helper"), None),
            P(("front", "helper"), None),
            P(("front", "helper")),
            P(("front", "helper")),
        ),
        out_specs=(P(("front", "helper"), None), P(("front", "helper"), None)),
        check_vma=False,
    )
```

```python
import functools

import jax
import jax.numpy as jnp
from jax import lax
from jax.experimental import pallas as pl
from jax.experimental.pallas import tpu as pltpu
from jax.sharding import PartitionSpec as P

UNIT = 128
SR = 4
PROWS = 128
BS = 128
NB = 16
NPIV = 2048
ROWS = 256
SLAB = 512
HELPERS = 128
CAP = 2
SLOTS = HELPERS * CAP
WIDE = SLAB + 128
ALL = SLAB + ROWS
F32 = jnp.float32
BF16 = jnp.bfloat16
NT = (((1,), (1,)), ((), ()))
TN = (((0,), (0,)), ((), ()))
LINE = 8
PAIRS = 4
SENT = NB - 1 + SR
PIECES = PAIRS * NB + 2 * NB
FROM = (0, 1, -1, 2, -2, 3, -3, 4)


def helper(y, z, core):
    return 2 * LINE * y + 2 * z + core


def line_groups():
    return [[helper(y, z, 0) for y in range(LINE)] for z in range(LINE)] + [
        [helper(g if z % 2 == 0 else 7 - g, z, 1) for z in range(LINE)] for g in range(LINE)
    ]


def from_offset(step):
    pairs = []
    for y in range(LINE):
        for z in range(LINE):
            pairs.append((helper(y, (z + step) % LINE, 0), helper(y, z, 0)))
            pairs.append((helper((y + step) % LINE, z, 1), helper(y, z, 1)))
    return pairs


def place():
    me = lax.axis_index("helper")
    return lax.div(me, 16), lax.rem(lax.div(me, 2), 8), lax.rem(me, 2)


def dot(a, b, dims=(((1,), (0,)), ((), ()))):
    return lax.dot_general(a, b, dims, preferred_element_type=F32)


def spread_kernel(panel_ref, rows_ref, out_ref, window):
    for j in range(NB):
        window[SR * j : SR * (j + 1), :] = rows_ref[:, BS * j : BS * (j + 1)].astype(F32)[:SR]
    leading = window[...].astype(BF16).reshape(SR, 16, BS)
    for d in range(LINE):
        for j in range(NB - 1):
            out_ref[d, j] = panel_ref[:, BS * j : BS * (j + 1)]
        out_ref[d, NB - 1 :] = leading


def spread_call(panel, rows):
    vmem = pl.BlockSpec(memory_space=pltpu.VMEM)
    return pl.pallas_call(
        spread_kernel,
        out_shape=jax.ShapeDtypeStruct((LINE, SENT, 16, BS), BF16),
        in_specs=[vmem, vmem],
        out_specs=vmem,
        scratch_shapes=[pltpu.VMEM((SR * NB, BS), F32)],
        compiler_params=pltpu.CompilerParams(allow_input_fusion=[False, True], vmem_limit_bytes=8 * 1024 * 1024),
        name="spread",
    )(panel, rows)


def pack_kernel(line_ref, out_ref, window):
    y, z, core = place()
    label = jnp.where(lax.rem(z, 2) == 0, y, 7 - y)
    low = jnp.minimum(label, 7 - label)
    for p in range(PAIRS):
        upper = jnp.where(core == 0, jnp.where(z >= 4, 1, 0), 1 if p >= 2 else 0)
        first = jnp.where(core == 0, p, low)
        count = 14 - 2 * first + upper
        swap = jnp.where(label <= 3, 0, 1)
        large = jnp.where(core == 0, 7 - p, 2 * p + 1 - swap)
        small = jnp.where(core == 0, p, 2 * p + swap)
        for s in range(NB):
            member = jnp.where(s < count, large, small)
            piece = jnp.where(s < count, s, s - count)
            out_ref[NB * p + s] = line_ref[member, piece]
    for d in range(LINE):
        leading = line_ref[d, NB - 1 :].astype(F32)
        for j in range(NB):
            window[j, SR * d : SR * (d + 1), :] = leading[j // 4, SR * (j % 4) : SR * (j % 4 + 1), :]
    out_ref[PAIRS * NB :] = window[...].astype(BF16).reshape(2 * NB, 16, BS)


def pack_call(line):
    vmem = pl.BlockSpec(memory_space=pltpu.VMEM)
    return pl.pallas_call(
        pack_kernel,
        out_shape=jax.ShapeDtypeStruct((PIECES, 16, BS), BF16),
        in_specs=[vmem],
        out_specs=vmem,
        scratch_shapes=[pltpu.VMEM((NB, SR * LINE, BS), F32)],
        compiler_params=pltpu.CompilerParams(vmem_limit_bytes=8 * 1024 * 1024),
        name="pack",
    )(line)


def held_at(step):
    place_of = jnp.int32(0)
    for q, offset in enumerate(FROM):
        place_of = jnp.where(step == (offset + LINE) % LINE, q, place_of)
    return PIECES * place_of


def put_tiles(first, second, y, z, lt, xw):
    for core, source in ((0, first), (1, second)):
        for member in range(LINE):
            if core == 0:
                base = held_at(lax.rem(member - z + LINE, LINE))
            else:
                at = jnp.where(lax.rem(z, 2) == 0, member, 7 - member)
                base = held_at(lax.rem(at - y + LINE, LINE))
            xw[core * LINE + member] = source[pl.ds(base + PAIRS * NB, 2 * NB)]
            for p in range(PAIRS):
                if core == 0:
                    low, upper = p, member // 4
                    large, small = helper(7 - p, member, 0), helper(p, member, 0)
                else:
                    low, upper = min(member, 7 - member), p // 2
                    z_large = 2 * p + 1 if member <= 3 else 2 * p
                    large, small = helper(7 - low, z_large, 1), helper(low, 4 * p + 1 - z_large, 1)
                count = 14 - 2 * low + upper
                lt[:count, large] = source[pl.ds(base + NB * p, count)]
                rest = 2 * low + upper
                if rest:
                    lt[:rest, small] = source[pl.ds(base + NB * p + count, rest)]


def prepare_kernel(count_ref, slot_ref, block_ref, held_ref, order_ref, chosen_ref, local_ref):
    live_count = UNIT * count_ref[0]
    held = lax.broadcasted_iota(jnp.int32, (1, SLAB), 1)
    group = lax.shift_right_logical(held, 5) & 7
    turn = lax.shift_right_logical(held, 2) & 7
    first_half = held < SLAB // 2
    held_y = jnp.where(first_half, turn, jnp.where((turn & 1) == 0, group, 7 - group))
    held_z = jnp.where(first_half, group, turn)
    column = 64 * held_y + 8 * held_z + jnp.where(first_half, 0, 4) + (held & 3)
    order = jnp.where(
        lax.broadcasted_iota(jnp.int32, (SLAB, SLAB), 0) == column, 1.0, 0.0
    ).astype(BF16)

    slot = slot_ref[...]
    owner_row = jnp.broadcast_to(lax.shift_right_logical(slot, 7).astype(F32), (ROWS, ROWS))
    owner_col = owner_row.T
    local_row = jnp.broadcast_to((slot & 127).astype(F32) + 1.0, (BS, ROWS))
    local_ref[...] = local_row.T.astype(BF16)
    i0 = lax.broadcasted_iota(jnp.int32, (ROWS, ROWS), 0)
    i1 = lax.broadcasted_iota(jnp.int32, (ROWS, ROWS), 1)
    earlier = jnp.where((owner_row == owner_col) & (i0 < i1) & (i0 < live_count), 1.0, 0.0)
    rank = jnp.sum(earlier, axis=0, keepdims=True)
    target = owner_row * CAP + rank
    chosen_ref[...] = jnp.where((target == i0.astype(F32)) & (i1 < live_count), 1.0, 0.0).astype(BF16)
    held_ref[...] = dot(block_ref[...], order)
    order_ref[...] = order


def prepare_call(count, slot, block):
    vmem = pl.BlockSpec(memory_space=pltpu.VMEM)
    return pl.pallas_call(
        prepare_kernel,
        out_shape=(
            jax.ShapeDtypeStruct((ROWS, SLAB), F32),
            jax.ShapeDtypeStruct((SLAB, SLAB), BF16),
            jax.ShapeDtypeStruct((SLOTS, ROWS), BF16),
            jax.ShapeDtypeStruct((ROWS, BS), BF16),
        ),
        in_specs=[pl.BlockSpec(memory_space=pltpu.SMEM), vmem, vmem],
        out_specs=(vmem,) * 4,
        compiler_params=pltpu.CompilerParams(vmem_limit_bytes=8 * 1024 * 1024),
        cost_estimate=pl.CostEstimate(flops=2 * ROWS * SLAB * SLAB, bytes_accessed=1 << 20, transcendentals=0),
        name="prepare",
    )(count, slot, block)


def front_kernel(
    count_ref, mine_ref, other_ref, rows_ref, inv_ref, block_ref, order_ref, chosen_ref, local_ref,
    factor_ref, send_ref, lt, xw, solved, wfac,
):
    y, z, core = place()

    @pl.when(core == 0)
    def _():
        put_tiles(mine_ref, other_ref, y, z, lt, xw)

    @pl.when(core == 1)
    def _():
        put_tiles(other_ref, mine_ref, y, z, lt, xw)

    live_count = UNIT * count_ref[0]
    live = lax.broadcasted_iota(jnp.int32, (ROWS, 1), 0) < live_count

    def window_piece(k):
        return xw[:, 2 * k : 2 * k + 2].reshape(SLAB, BS)

    def panel_piece(j, top, count):
        return lt[j, top // 16 : (top + count) // 16].reshape(count, BS)

    def start_block(k):
        return jnp.concatenate([window_piece(k), rows_ref[:, BS * k : BS * (k + 1)]], axis=0).astype(F32)

    def scale(part, k):
        f = dot(part, inv_ref[k]).astype(BF16)
        wfac[:, BS * k : BS * (k + 1)] = f[:SLAB]
        factor_ref[:, BS * k : BS * (k + 1)] = jnp.where(live, f[SLAB:], jnp.zeros((), BF16))

    def pair(s):
        return jnp.concatenate([start_block(2 * s), start_block(2 * s + 1)], axis=1)

    groups = ((0, 512), (512, 768))

    def start_rows(k, g):
        r0, r1 = groups[g]
        parts = []
        if r0 < SLAB:
            parts.append(window_piece(k)[r0 : min(r1, SLAB)])
        if r1 > SLAB:
            parts.append(rows_ref[max(r0, SLAB) - SLAB : r1 - SLAB, BS * k : BS * (k + 1)])
        return jnp.concatenate(parts, axis=0).astype(F32)

    def pair2(s, g):
        return jnp.concatenate([start_rows(2 * s, g), start_rows(2 * s + 1, g)], axis=1)

    pend = [pair2(0, g) for g in range(len(groups))]
    lasts = [None] * len(groups)
    for s in range(NB // 2):
        lo = 256 * s
        k0, k1 = 2 * s, 2 * s + 1
        xs = list(pend)
        if s > 0:
            panel = jnp.concatenate([panel_piece(j, lo, 256) for j in (k0 - 2, k0 - 1)], axis=1)
            xs = [xs[g] - dot(lasts[g], panel, NT) for g in range(len(groups))]
        s0s = [x[:, :BS].astype(BF16) for x in xs]
        if s + 1 < NB // 2:
            pend = [pair2(s + 1, g) for g in range(len(groups))]
            if s > 0:
                panel = jnp.concatenate([panel_piece(j, lo + 256, 256) for j in range(k0)], axis=1)
                pend = [pend[g] - dot(solved[r0:r1, :lo], panel, NT) for g, (r0, r1) in enumerate(groups)]
        diag = panel_piece(k0, lo + BS, BS)
        s1s = [(xs[g][:, BS:] - dot(s0s[g], diag, NT)).astype(BF16) for g in range(len(groups))]
        lasts = [jnp.concatenate([s0s[g], s1s[g]], axis=1) for g in range(len(groups))]
        for g, (r0, r1) in enumerate(groups):
            solved[r0:r1, lo : lo + 256] = lasts[g]
        scale(jnp.concatenate(s0s, axis=0), k0)
        scale(jnp.concatenate(s1s, axis=0), k1)

    product = dot(solved[SLAB:, :], wfac[...], NT)
    held_contribution = jnp.where(live, block_ref[...] - product, 0.0).astype(BF16)
    contribution = dot(held_contribution, order_ref[...], NT).astype(BF16)

    payload = jnp.concatenate([contribution, local_ref[...]], axis=1)
    send_ref[...] = dot(chosen_ref[...], payload).astype(BF16)


def front_call(mine, other, rows, inverse, count, prepared):
    vmem = pl.BlockSpec(memory_space=pltpu.VMEM)
    return pl.pallas_call(
        front_kernel,
        out_shape=(
            jax.ShapeDtypeStruct((ROWS, NPIV), BF16),
            jax.ShapeDtypeStruct((SLOTS, WIDE), BF16),
        ),
        in_specs=[pl.BlockSpec(memory_space=pltpu.SMEM)] + [vmem] * 8,
        out_specs=(vmem, vmem),
        scratch_shapes=[
            pltpu.VMEM((NB, HELPERS, 16, BS), BF16),
            pltpu.VMEM((2 * LINE, 2 * NB, 16, BS), BF16),
            pltpu.VMEM((ALL, NPIV), BF16),
            pltpu.VMEM((SLAB, NPIV), BF16),
        ],
        compiler_params=pltpu.CompilerParams(vmem_limit_bytes=32 * 1024 * 1024),
        name="front",
    )(count, mine, other, rows, inverse, *prepared)


def assemble_kernel(got_ref, out_ref):
    got = got_ref[...]
    local = got[:, SLAB:].astype(F32)
    wanted = lax.broadcasted_iota(jnp.int32, (SLOTS, PROWS), 1).astype(F32) + 1.0
    chooser = jnp.where(local == wanted, 1.0, 0.0).astype(BF16)
    out_ref[...] = dot(chooser, got[:, :SLAB], TN)


def assemble_call(got):
    vmem = pl.BlockSpec(memory_space=pltpu.VMEM)
    return pl.pallas_call(
        assemble_kernel,
        out_shape=jax.ShapeDtypeStruct((PROWS, SLAB), F32),
        in_specs=[vmem],
        out_specs=vmem,
        compiler_params=pltpu.CompilerParams(vmem_limit_bytes=8 * 1024 * 1024),
        name="assemble",
    )(got)


def per_device(lower_panel, pivot_inverse, lower_rows, window_block, block_count, parent_slot):
    def receive(block, step):
        return lax.ppermute(block, "helper", from_offset(step))

    line = lax.all_to_all(
        spread_call(lower_panel, lower_rows[:16]), "helper", 0, 0, tiled=True, axis_index_groups=line_groups()
    )
    own = pack_call(line)
    half = PIECES // 2
    up, down = receive(own, 1), receive(own, -1)
    up2, down2 = receive(own, 2), receive(own, -2)
    mine = jnp.concatenate(
        [own, up, down, up2, down2]
        + [receive(up2, 1), receive(down2, -1), receive(up2[:half], 2), receive(down2[half:], -2)]
    )
    other = lax.ppermute(mine, "helper", [(h, h ^ 1) for h in range(HELPERS)])
    factor, send = front_call(
        mine, other, lower_rows, pivot_inverse, block_count,
        prepare_call(block_count, parent_slot.reshape(1, ROWS), window_block),
    )
    got = lax.all_to_all(
        send.reshape(HELPERS, CAP, WIDE), "helper", split_axis=0, concat_axis=0, tiled=True
    )
    return factor, assemble_call(got.reshape(SLOTS, WIDE))


def solution(mesh):
    return jax.shard_map(
        per_device,
        mesh=mesh,
        in_specs=(
            P(("front", "helper"), None),
            P("front", None, None),
            P(("front", "helper"), None),
            P(("front", "helper"), None),
            P(("front", "helper")),
            P(("front", "helper")),
        ),
        out_specs=(P(("front", "helper"), None), P(("front", "helper"), None)),
        check_vma=False,
    )
```

```python
import functools

import jax
import jax.numpy as jnp
from jax import lax
from jax.experimental import pallas as pl
from jax.experimental.pallas import tpu as pltpu
from jax.sharding import PartitionSpec as P

UNIT = 128
SR = 4
PROWS = 128
BS = 128
NB = 16
NPIV = 2048
ROWS = 256
SLAB = 512
HELPERS = 128
CAP = 2
SLOTS = HELPERS * CAP
WIDE = SLAB + 128
ALL = SLAB + ROWS
F32 = jnp.float32
BF16 = jnp.bfloat16
NT = (((1,), (1,)), ((), ()))
TN = (((0,), (0,)), ((), ()))
LINE = 8
PAIRS = 4
SENT = NB - 1 + SR
PIECES = PAIRS * NB + 2 * NB
FROM = (0, 1, -1, 2, -2, 3, -3, 4)


def helper(y, z, core):
    return 2 * LINE * y + 2 * z + core


def line_groups():
    return [[helper(y, z, 0) for y in range(LINE)] for z in range(LINE)] + [
        [helper(g if z % 2 == 0 else 7 - g, z, 1) for z in range(LINE)] for g in range(LINE)
    ]


def from_offset(step):
    pairs = []
    for y in range(LINE):
        for z in range(LINE):
            pairs.append((helper(y, (z + step) % LINE, 0), helper(y, z, 0)))
            pairs.append((helper((y + step) % LINE, z, 1), helper(y, z, 1)))
    return pairs


def place():
    me = lax.axis_index("helper")
    return lax.div(me, 16), lax.rem(lax.div(me, 2), 8), lax.rem(me, 2)


def dot(a, b, dims=(((1,), (0,)), ((), ()))):
    return lax.dot_general(a, b, dims, preferred_element_type=F32)


def spread_kernel(held_ref, out_ref, window):
    for j in range(NB):
        window[SR * j : SR * (j + 1), :] = held_ref[16:, BS * j : BS * (j + 1)].astype(F32)[:SR]
    leading = window[...].astype(BF16).reshape(SR, 16, BS)
    for d in range(LINE):
        for j in range(NB - 1):
            out_ref[d, j] = held_ref[:16, BS * j : BS * (j + 1)]
        out_ref[d, NB - 1 :] = leading


def spread_call(held):
    vmem = pl.BlockSpec(memory_space=pltpu.VMEM)
    return pl.pallas_call(
        spread_kernel,
        out_shape=jax.ShapeDtypeStruct((LINE, SENT, 16, BS), BF16),
        in_specs=[vmem],
        out_specs=vmem,
        scratch_shapes=[pltpu.VMEM((SR * NB, BS), F32)],
        compiler_params=pltpu.CompilerParams(vmem_limit_bytes=8 * 1024 * 1024),
        name="spread",
    )(held)


def pack_kernel(line_ref, out_ref, window):
    y, z, core = place()
    label = jnp.where(lax.rem(z, 2) == 0, y, 7 - y)
    low = jnp.minimum(label, 7 - label)
    for p in range(PAIRS):
        upper = jnp.where(core == 0, jnp.where(z >= 4, 1, 0), 1 if p >= 2 else 0)
        first = jnp.where(core == 0, p, low)
        count = 14 - 2 * first + upper
        swap = jnp.where(label <= 3, 0, 1)
        large = jnp.where(core == 0, 7 - p, 2 * p + 1 - swap)
        small = jnp.where(core == 0, p, 2 * p + swap)
        for s in range(NB):
            member = jnp.where(s < count, large, small)
            piece = jnp.where(s < count, s, s - count)
            out_ref[NB * p + s] = line_ref[member, piece]
    for d in range(LINE):
        leading = line_ref[d, NB - 1 :].astype(F32)
        for j in range(NB):
            window[j, SR * d : SR * (d + 1), :] = leading[j // 4, SR * (j % 4) : SR * (j % 4 + 1), :]
    out_ref[PAIRS * NB :] = window[...].astype(BF16).reshape(2 * NB, 16, BS)


def pack_call(line):
    vmem = pl.BlockSpec(memory_space=pltpu.VMEM)
    return pl.pallas_call(
        pack_kernel,
        out_shape=jax.ShapeDtypeStruct((PIECES, 16, BS), BF16),
        in_specs=[vmem],
        out_specs=vmem,
        scratch_shapes=[pltpu.VMEM((NB, SR * LINE, BS), F32)],
        compiler_params=pltpu.CompilerParams(vmem_limit_bytes=8 * 1024 * 1024),
        name="pack",
    )(line)


def held_at(step):
    place_of = jnp.int32(0)
    for q, offset in enumerate(FROM):
        place_of = jnp.where(step == (offset + LINE) % LINE, q, place_of)
    return PIECES * place_of


def put_tiles(first, second, y, z, lt, xw):
    for core, source in ((0, first), (1, second)):
        for member in range(LINE):
            if core == 0:
                base = held_at(lax.rem(member - z + LINE, LINE))
            else:
                at = jnp.where(lax.rem(z, 2) == 0, member, 7 - member)
                base = held_at(lax.rem(at - y + LINE, LINE))
            xw[core * LINE + member] = source[pl.ds(base + PAIRS * NB, 2 * NB)]
            for p in range(PAIRS):
                if core == 0:
                    low, upper = p, member // 4
                    large, small = helper(7 - p, member, 0), helper(p, member, 0)
                else:
                    low, upper = min(member, 7 - member), p // 2
                    z_large = 2 * p + 1 if member <= 3 else 2 * p
                    large, small = helper(7 - low, z_large, 1), helper(low, 4 * p + 1 - z_large, 1)
                count = 14 - 2 * low + upper
                lt[:count, large] = source[pl.ds(base + NB * p, count)]
                rest = 2 * low + upper
                if rest:
                    lt[:rest, small] = source[pl.ds(base + NB * p + count, rest)]


def prepare_kernel(count_ref, slot_ref, block_ref, held_ref, order_ref, chosen_ref, local_ref):
    live_count = UNIT * count_ref[0]
    held = lax.broadcasted_iota(jnp.int32, (1, SLAB), 1)
    group = lax.shift_right_logical(held, 5) & 7
    turn = lax.shift_right_logical(held, 2) & 7
    first_half = held < SLAB // 2
    held_y = jnp.where(first_half, turn, jnp.where((turn & 1) == 0, group, 7 - group))
    held_z = jnp.where(first_half, group, turn)
    column = 64 * held_y + 8 * held_z + jnp.where(first_half, 0, 4) + (held & 3)
    order = jnp.where(
        lax.broadcasted_iota(jnp.int32, (SLAB, SLAB), 0) == column, 1.0, 0.0
    ).astype(BF16)

    slot = slot_ref[...]
    owner_row = jnp.broadcast_to(lax.shift_right_logical(slot, 7).astype(F32), (ROWS, ROWS))
    owner_col = owner_row.T
    local_row = jnp.broadcast_to((slot & 127).astype(F32) + 1.0, (BS, ROWS))
    local_ref[...] = local_row.T.astype(BF16)
    i0 = lax.broadcasted_iota(jnp.int32, (ROWS, ROWS), 0)
    i1 = lax.broadcasted_iota(jnp.int32, (ROWS, ROWS), 1)
    earlier = jnp.where((owner_row == owner_col) & (i0 < i1) & (i0 < live_count), 1.0, 0.0)
    rank = jnp.sum(earlier, axis=0, keepdims=True)
    target = owner_row * CAP + rank
    chosen_ref[...] = jnp.where((target == i0.astype(F32)) & (i1 < live_count), 1.0, 0.0).astype(BF16)
    held_ref[...] = dot(block_ref[...], order)
    order_ref[...] = order


def prepare_call(count, slot, block):
    vmem = pl.BlockSpec(memory_space=pltpu.VMEM)
    return pl.pallas_call(
        prepare_kernel,
        out_shape=(
            jax.ShapeDtypeStruct((ROWS, SLAB), F32),
            jax.ShapeDtypeStruct((SLAB, SLAB), BF16),
            jax.ShapeDtypeStruct((SLOTS, ROWS), BF16),
            jax.ShapeDtypeStruct((ROWS, BS), BF16),
        ),
        in_specs=[pl.BlockSpec(memory_space=pltpu.SMEM), vmem, vmem],
        out_specs=(vmem,) * 4,
        compiler_params=pltpu.CompilerParams(vmem_limit_bytes=8 * 1024 * 1024),
        cost_estimate=pl.CostEstimate(flops=2 * ROWS * SLAB * SLAB, bytes_accessed=1 << 20, transcendentals=0),
        name="prepare",
    )(count, slot, block)


def front_kernel(
    count_ref, mine_ref, other_ref, rows_ref, inv_ref, block_ref, order_ref, chosen_ref, local_ref,
    factor_ref, send_ref, lt, xw, solved, wfac,
):
    y, z, core = place()

    @pl.when(core == 0)
    def _():
        put_tiles(mine_ref, other_ref, y, z, lt, xw)

    @pl.when(core == 1)
    def _():
        put_tiles(other_ref, mine_ref, y, z, lt, xw)

    live_count = UNIT * count_ref[0]
    live = lax.broadcasted_iota(jnp.int32, (ROWS, 1), 0) < live_count

    def window_piece(k):
        return xw[:, 2 * k : 2 * k + 2].reshape(SLAB, BS)

    def panel_piece(j, top, count):
        return lt[j, top // 16 : (top + count) // 16].reshape(count, BS)

    def start_block(k):
        return jnp.concatenate([window_piece(k), rows_ref[:, BS * k : BS * (k + 1)]], axis=0).astype(F32)

    def scale(part, k):
        f = dot(part, inv_ref[k]).astype(BF16)
        wfac[:, BS * k : BS * (k + 1)] = f[:SLAB]
        factor_ref[:, BS * k : BS * (k + 1)] = jnp.where(live, f[SLAB:], jnp.zeros((), BF16))

    def pair(s):
        return jnp.concatenate([start_block(2 * s), start_block(2 * s + 1)], axis=1)

    groups = ((512, 768), (0, 512))

    def start_rows(k, g):
        r0, r1 = groups[g]
        parts = []
        if r0 < SLAB:
            parts.append(window_piece(k)[r0 : min(r1, SLAB)])
        if r1 > SLAB:
            parts.append(rows_ref[max(r0, SLAB) - SLAB : r1 - SLAB, BS * k : BS * (k + 1)])
        return jnp.concatenate(parts, axis=0).astype(F32)

    def pair2(s, g):
        return jnp.concatenate([start_rows(2 * s, g), start_rows(2 * s + 1, g)], axis=1)

    pend = [pair2(0, g) for g in range(len(groups))]
    lasts = [None] * len(groups)
    for s in range(NB // 2):
        lo = 256 * s
        k0, k1 = 2 * s, 2 * s + 1
        xs = list(pend)
        if s > 0:
            panel = jnp.concatenate([panel_piece(j, lo, 256) for j in (k0 - 2, k0 - 1)], axis=1)
            xs = [xs[g] - dot(lasts[g], panel, NT) for g in range(len(groups))]
        s0s = [x[:, :BS].astype(BF16) for x in xs]
        if s + 1 < NB // 2:
            pend = [pair2(s + 1, g) for g in range(len(groups))]
            if s > 0:
                panel = jnp.concatenate([panel_piece(j, lo + 256, 256) for j in range(k0)], axis=1)
                pend = [pend[g] - dot(solved[r0:r1, :lo], panel, NT) for g, (r0, r1) in enumerate(groups)]
        diag = panel_piece(k0, lo + BS, BS)
        s1s = [(xs[g][:, BS:] - dot(s0s[g], diag, NT)).astype(BF16) for g in range(len(groups))]
        lasts = [jnp.concatenate([s0s[g], s1s[g]], axis=1) for g in range(len(groups))]
        for g, (r0, r1) in enumerate(groups):
            solved[r0:r1, lo : lo + 256] = lasts[g]
        scale(jnp.concatenate(s0s[::-1], axis=0), k0)
        scale(jnp.concatenate(s1s[::-1], axis=0), k1)

    product = dot(solved[SLAB:, :], wfac[...], NT)
    held_contribution = jnp.where(live, block_ref[...] - product, 0.0).astype(BF16)
    contribution = dot(held_contribution, order_ref[...], NT).astype(BF16)

    payload = jnp.concatenate([contribution, local_ref[...]], axis=1)
    send_ref[...] = dot(chosen_ref[...], payload).astype(BF16)


def front_call(mine, other, rows, inverse, count, prepared):
    vmem = pl.BlockSpec(memory_space=pltpu.VMEM)
    return pl.pallas_call(
        front_kernel,
        out_shape=(
            jax.ShapeDtypeStruct((ROWS, NPIV), BF16),
            jax.ShapeDtypeStruct((SLOTS, WIDE), BF16),
        ),
        in_specs=[pl.BlockSpec(memory_space=pltpu.SMEM)] + [vmem] * 8,
        out_specs=(vmem, vmem),
        scratch_shapes=[
            pltpu.VMEM((NB, HELPERS, 16, BS), BF16),
            pltpu.VMEM((2 * LINE, 2 * NB, 16, BS), BF16),
            pltpu.VMEM((ALL, NPIV), BF16),
            pltpu.VMEM((SLAB, NPIV), BF16),
        ],
        compiler_params=pltpu.CompilerParams(vmem_limit_bytes=32 * 1024 * 1024),
        name="front",
    )(count, mine, other, rows, inverse, *prepared)


def assemble_kernel(got_ref, out_ref):
    got = got_ref[...]
    local = got[:, SLAB:].astype(F32)
    wanted = lax.broadcasted_iota(jnp.int32, (SLOTS, PROWS), 1).astype(F32) + 1.0
    chooser = jnp.where(local == wanted, 1.0, 0.0).astype(BF16)
    out_ref[...] = dot(chooser, got[:, :SLAB], TN)


def assemble_call(got):
    vmem = pl.BlockSpec(memory_space=pltpu.VMEM)
    return pl.pallas_call(
        assemble_kernel,
        out_shape=jax.ShapeDtypeStruct((PROWS, SLAB), F32),
        in_specs=[vmem],
        out_specs=vmem,
        compiler_params=pltpu.CompilerParams(vmem_limit_bytes=8 * 1024 * 1024),
        name="assemble",
    )(got)


def per_device(lower_panel, pivot_inverse, lower_rows, window_block, block_count, parent_slot):
    def receive(block, step):
        return lax.ppermute(block, "helper", from_offset(step))

    line = lax.all_to_all(
        spread_call(jnp.concatenate([lower_panel, lower_rows[:16]])), "helper", 0, 0, tiled=True, axis_index_groups=line_groups()
    )
    own = pack_call(line)
    half = PIECES // 2
    up, down = receive(own, 1), receive(own, -1)
    up2, down2 = receive(own, 2), receive(own, -2)
    mine = jnp.concatenate(
        [own, up, down, up2, down2]
        + [receive(up2, 1), receive(down2, -1), receive(up2[:half], 2), receive(down2[half:], -2)]
    )
    other = lax.ppermute(mine, "helper", [(h, h ^ 1) for h in range(HELPERS)])
    factor, send = front_call(
        mine, other, lower_rows, pivot_inverse, block_count,
        prepare_call(block_count, parent_slot.reshape(1, ROWS), window_block),
    )
    got = lax.all_to_all(
        send.reshape(HELPERS, CAP, WIDE), "helper", split_axis=0, concat_axis=0, tiled=True
    )
    return factor, assemble_call(got.reshape(SLOTS, WIDE))


def solution(mesh):
    return jax.shard_map(
        per_device,
        mesh=mesh,
        in_specs=(
            P(("front", "helper"), None),
            P("front", None, None),
            P(("front", "helper"), None),
            P(("front", "helper"), None),
            P(("front", "helper")),
            P(("front", "helper")),
        ),
        out_specs=(P(("front", "helper"), None), P(("front", "helper"), None)),
        check_vma=False,
    )
```
